32 devices in a mesh: dp: 16 (over z, y, x), mp: 2 (over core).
Axes of the slice: x: 2, y: 2, z: 4, core: 2. Of those that a mesh axis runs over, the one named last changes fastest.
Arguments:
- query_emb: bfloat16 [128, 4096], P('dp', 'mp'), as said below
- item_emb: bfloat16 [128, 4096], P('dp', 'mp'), as said below
- pair_index: int32 [128], P('dp'), may hold values from 0 to 127, each once
- hard_index: int32 [128, 4], P('dp'), may hold values from 0 to 127
- hidden_in: bfloat16 [2, 16, 152, 4096], P(None, 'dp', None, 'mp'), may hold values from -24 to 24
- lengths: int32 [2, 16], P(None, 'dp'), may hold values from 76 to 152
- w_query: bfloat16 [4096, 4096], P('dp', 'mp'), as said below
- key_weight_matrix: bfloat16 [4096, 1024], P(None, 'mp'), as said below
- value_weight_matrix: bfloat16 [4096, 1024], P(None, 'mp'), may hold values from -0.09375 to 0.09375
- w_out: bfloat16 [4096, 4096], P('mp', 'dp'), may hold values from -0.09375 to 0.09375
- key_down_matrix: bfloat16 [4096, 16], replicated, may hold values from -0.09375 to 0.09375
- key_up_matrix: bfloat16 [16, 1024], P(None, 'mp'), may hold values from -0.29882812 to 0.29882812
- value_down: bfloat16 [4096, 16], replicated, may hold values from -0.09375 to 0.09375
- value_up_matrix: bfloat16 [16, 1024], P(None, 'mp'), may hold values from -0.29882812 to 0.29882812
Outputs:
- mean_loss: float32 [], replicated
- query_grad: bfloat16 [128, 4096], P('dp', 'mp')
- item_grad: bfloat16 [128, 4096], P('dp', 'mp')
- input_grad: bfloat16 [2, 16, 152, 4096], P(None, 'dp', None, 'mp')
- key_down_grad: float32 [4096, 16], replicated
- value_down_grad: float32 [4096, 16], replicated
- key_up_grad: float32 [16, 1024], P(None, 'mp')
- value_up_grad: float32 [16, 1024], P(None, 'mp')
The draws below stay inside these ranges and needn't reach their ends.
Inputs may be any that keep to these rules, and one draw needn't show every extreme that they name: `query_emb`: entries within 10 / sqrt(4096) in magnitude. `item_emb`: entries within 10 / sqrt(4096) in magnitude. `w_query`: entries within 16 / sqrt(4096) in magnitude. `key_weight_matrix`: entries within 6 / sqrt(4096) in magnitude.
All inputs are finite; a program needn't handle non-finite values.
Results may differ from the reference program's by a relative error of at most 0.025.
The reference program's roundings to bfloat16 on the way count: a program that leaves them out, or rounds other values in their place, can miss the bound.
Values may be sent and summed in bfloat16 or wider, within the bound.
A program may use at most 128 MiB of HBM per device.

```python
import math
import jax
import jax.numpy as jnp
from jax import lax

D = 4096
HEADS = 32
KV_HEADS = 8
HEAD_DIM = 128
RANK = 16
HARD = 4
SUBS = 2
B_DEV = 8
LEN = 152
BATCH = 128
SEQS = 16
N_MP = 2


def draw_rows(base_key):
    normal_part = jnp.clip(jax.random.normal(jax.random.fold_in(base_key, 1), (BATCH, D)), -6.0, 6.0)
    return normal_part / math.sqrt(D)


def embed_pair(key):
    queries = draw_rows(jax.random.fold_in(key, 11))
    items = draw_rows(jax.random.fold_in(key, 12))
    anchors = jnp.array([0, BATCH // 3, 2 * BATCH // 3, BATCH - 1], dtype=jnp.int32)
    for offset, lowered in ((1, 0.0), (BATCH // 2, 0.04)):
        targets = (anchors + offset) % BATCH
        blended = items[targets]
        items = items.at[targets].set(blended)
    return (queries, items)


def draw_query_emb(key, part):
    queries, items = embed_pair(key)
    return queries.astype(jnp.bfloat16)


def draw_item_emb(key, part):
    queries, items = embed_pair(key)
    return items.astype(jnp.bfloat16)


def key_basis(key):
    return jnp.clip(jax.random.normal(jax.random.fold_in(key, 21), (D, KV_HEADS * HEAD_DIM)), -6.0, 6.0)


def draw_key_weight_matrix(key, part):
    basis = key_basis(key)
    return (basis / math.sqrt(D)).astype(jnp.bfloat16)


def draw_w_query(key, part):
    key = jax.random.fold_in(key, 6)
    own_part = jnp.clip(jax.random.normal(key, (D, HEADS * HEAD_DIM)), -6.0, 6.0)
    mixed = own_part
    return (mixed / math.sqrt(D)).astype(jnp.bfloat16)


def draw_hidden_in(key, part):
    key = jax.random.fold_in(key, 7)
    extent = (SUBS, SEQS, LEN, D)
    normal_part = jnp.clip(jax.random.normal(jax.random.fold_in(key, 1), extent), -6.0, 6.0)
    seq_order = jnp.arange(SEQS, dtype=jnp.int32)[None, :] * SUBS + jnp.arange(SUBS, dtype=jnp.int32)[:, None]
    heavy_column = (seq_order % D).reshape(SUBS, SEQS, 1, 1)
    feature_ids = jnp.arange(D, dtype=jnp.int32).reshape(1, 1, 1, D)
    heavy = 14.0 * (feature_ids == heavy_column).astype(jnp.float32)
    mixed = normal_part + heavy
    return jnp.clip(mixed, -24.0, 24.0).astype(jnp.bfloat16)


def draw_lengths(key, part):
    key = jax.random.fold_in(key, 9)
    drawn = jax.random.randint(key, (SUBS, SEQS), LEN // 2, LEN + 1)
    return drawn.at[0, 0].set(LEN).astype(jnp.int32)


def set_ends(entries, rng, least, largest):
    longest = entries.shape.index(max(entries.shape))
    spots = []
    for shift in (0, 1):
        where = [jax.random.randint(jax.random.fold_in(rng, axis), (), 0, length) for axis, length in enumerate(entries.shape)]
        where[longest] = (where[longest] + shift) % entries.shape[longest]
        spots.append(tuple(where))
    return entries.at[spots[0]].set(least).at[spots[1]].set(largest)


def shard_levels(stream_key, dims, pieces, least, top_value):
    gain = 1.0
    for position, shards_of in pieces:
        heights = jax.random.uniform(jax.random.fold_in(jax.random.fold_in(stream_key, 6), position), (shards_of,), jnp.float32, least / len(pieces), top_value / len(pieces))
        gain = gain * jnp.repeat(jnp.exp(heights), dims[position] // shards_of).reshape((-1,) + (1,) * (len(dims) - 1 - position))
    return gain


def noise(stream_key, shape, scale, reach, shards=(), kind=jnp.bfloat16):
    values = scale * jax.random.normal(stream_key, shape, jnp.float32)
    if shards:
        values = values * shard_levels(stream_key, shape, shards, -0.22, 0.18)
    return jnp.clip(values, -reach, reach).astype(kind)


def setup_inputs(seed: int = 0) -> dict:
    key_of = jax.random.split(jax.random.key(seed), 15)
    query_emb = draw_query_emb(jax.random.fold_in(key_of[14], 71), 0)
    item_emb = draw_item_emb(jax.random.fold_in(key_of[14], 71), 0)
    pair_index = jax.random.permutation(key_of[2], BATCH).astype(jnp.int32)
    hard_index = set_ends(jax.random.randint(key_of[3], (BATCH, HARD), 0, BATCH), jax.random.fold_in(key_of[3], 1), 0, BATCH - 1).astype(jnp.int32)
    hidden_in = draw_hidden_in(jax.random.fold_in(key_of[14], 71), 0)
    lengths = draw_lengths(jax.random.fold_in(key_of[14], 71), 0)
    w_query = draw_w_query(jax.random.fold_in(key_of[14], 71), 0)
    key_weight_matrix = draw_key_weight_matrix(jax.random.fold_in(key_of[14], 71), 0)
    value_weight_matrix = noise(key_of[8], (D, KV_HEADS * HEAD_DIM), D ** -0.5, 0.09375, ((1, 2),))
    w_out = noise(key_of[9], (HEADS * HEAD_DIM, D), (HEADS * HEAD_DIM) ** -0.5, 0.09375, ((0, 2), (1, 16)))
    key_down_matrix = noise(key_of[10], (D, RANK), D ** -0.5, 0.09375)
    key_up_matrix = noise(key_of[11], (RANK, KV_HEADS * HEAD_DIM), 0.05, 0.29882812, ((1, 2),))
    value_down = noise(key_of[12], (D, RANK), D ** -0.5, 0.09375)
    value_up_matrix = noise(key_of[13], (RANK, KV_HEADS * HEAD_DIM), 0.05, 0.29882812, ((1, 2),))
    return {"query_emb": query_emb, "item_emb": item_emb, "pair_index": pair_index, "hard_index": hard_index, "hidden_in": hidden_in, "lengths": lengths, "w_query": w_query, "key_weight_matrix": key_weight_matrix, "value_weight_matrix": value_weight_matrix, "w_out": w_out, "key_down_matrix": key_down_matrix, "key_up_matrix": key_up_matrix, "value_down": value_down, "value_up_matrix": value_up_matrix}


INV_TEMP = 50.0
HARD_NEGATIVE_ADD = 4.0
ADAPTER_SCALE = 2.0

def final_product(left_side, right_side):
    return lax.dot_general(left_side, right_side, (((1,), (1,)), ((), ())), preferred_element_type=jnp.float32)

def first_product(left_side, right_side):
    return lax.dot_general(left_side, right_side, (((0,), (0,)), ((), ())), preferred_element_type=jnp.float32)

def rounded(value):
    return lax.optimization_barrier(value.astype(jnp.bfloat16)).astype(jnp.float32)

def reference(query_emb, item_emb, pair_index, hard_index, hidden_in, lengths, w_query, key_weight_matrix, value_weight_matrix, w_out, key_down_matrix, key_up_matrix, value_down, value_up_matrix):
    columns = jnp.arange(BATCH, dtype=jnp.int32)
    pair_scores = final_product(query_emb, item_emb) * INV_TEMP
    hard_negative_count = lax.optimization_barrier(jnp.sum((hard_index[:, :, None] == columns[None, None, :]).astype(jnp.float32), axis=1))
    score_logits = pair_scores + HARD_NEGATIVE_ADD * hard_negative_count
    row_top = lax.optimization_barrier(jnp.max(score_logits, axis=1, keepdims=True))
    log_total = row_top[:, 0] + jnp.log(lax.optimization_barrier(jnp.sum(jnp.exp(score_logits - row_top), axis=1)))
    target = (pair_index[:, None] == columns[None, :]).astype(jnp.float32)
    picked = lax.optimization_barrier(jnp.sum(target * score_logits, axis=1))
    mean_loss = jnp.sum(log_total - picked) / BATCH
    residual = (jnp.exp(score_logits - log_total[:, None]) - target).astype(jnp.bfloat16)
    query_grad = (jnp.dot(residual, item_emb, preferred_element_type=jnp.float32) * INV_TEMP).astype(jnp.bfloat16)
    item_grad = (first_product(residual, query_emb) * INV_TEMP).astype(jnp.bfloat16)
    group_size = HEADS // KV_HEADS
    key_width = KV_HEADS * HEAD_DIM // N_MP
    query_width = HEADS * HEAD_DIM // N_MP
    score_scale = 1.0 / math.sqrt(HEAD_DIM)
    flat_x = hidden_in.reshape(SUBS * SEQS, LEN, D)
    flat_len = lengths.reshape(SUBS * SEQS)
    seq_ids = jnp.arange(SUBS * SEQS, dtype=jnp.int32)
    item_rows = seq_ids % SEQS * B_DEV + seq_ids // SEQS
    cotangents = jnp.take(item_grad, item_rows, axis=0)
    key_down_float = key_down_matrix.astype(jnp.float32)
    value_down_float = value_down.astype(jnp.float32)

    def one_sequence(state_sum, packed):
        token_inputs, length, cotangent = packed
        reduced_key = jnp.dot(token_inputs, key_down_matrix, preferred_element_type=jnp.float32).astype(jnp.bfloat16)
        reduced_value = jnp.dot(token_inputs, value_down, preferred_element_type=jnp.float32).astype(jnp.bfloat16)
        key_rows = (jnp.dot(token_inputs, key_weight_matrix, preferred_element_type=jnp.float32) + ADAPTER_SCALE * jnp.dot(reduced_key, key_up_matrix, preferred_element_type=jnp.float32)).astype(jnp.bfloat16)
        value_rows = (jnp.dot(token_inputs, value_weight_matrix, preferred_element_type=jnp.float32) + ADAPTER_SCALE * jnp.dot(reduced_value, value_up_matrix, preferred_element_type=jnp.float32)).astype(jnp.bfloat16)
        last_tokens = lax.dynamic_slice_in_dim(token_inputs, (length - 1).astype(jnp.int32), 1, 0)
        query = jnp.dot(last_tokens, w_query, preferred_element_type=jnp.float32).astype(jnp.bfloat16)
        q_heads = query.reshape(KV_HEADS, group_size, HEAD_DIM).astype(jnp.float32)
        k_heads = key_rows.reshape(LEN, KV_HEADS, HEAD_DIM).astype(jnp.float32)
        v_heads = value_rows.reshape(LEN, KV_HEADS, HEAD_DIM).astype(jnp.float32)
        raw_scores = jnp.einsum('kgd,jkd->kgj', q_heads, k_heads) * score_scale
        live_mask = jnp.arange(LEN, dtype=jnp.int32) < length
        raw_scores = jnp.where(live_mask[None, None, :], raw_scores, -jnp.inf)
        row_peak = lax.optimization_barrier(jnp.max(raw_scores, axis=-1, keepdims=True))
        weights = jnp.exp(raw_scores - row_peak)
        softmax_probs = weights / lax.optimization_barrier(jnp.sum(weights, axis=-1, keepdims=True))
        attn_grad = final_product(cotangent[None, :], w_out).astype(jnp.bfloat16)
        grad_heads = attn_grad.reshape(KV_HEADS, group_size, HEAD_DIM).astype(jnp.float32)
        prob_grad = jnp.einsum('kgd,jkd->kgj', grad_heads, v_heads)
        score_grad = rounded(softmax_probs * (prob_grad - lax.optimization_barrier(jnp.sum(softmax_probs * prob_grad, axis=-1, keepdims=True))) * score_scale)
        query_delta = jnp.einsum('kgj,jkd->kgd', score_grad, k_heads).astype(jnp.bfloat16).reshape(1, HEADS * HEAD_DIM)
        key_adapter_change = jnp.einsum('kgj,kgd->jkd', score_grad, q_heads).astype(jnp.bfloat16).reshape(LEN, KV_HEADS * HEAD_DIM)
        value_adapter_change = jnp.einsum('kgj,kgd->jkd', rounded(softmax_probs), grad_heads).astype(jnp.bfloat16).reshape(LEN, KV_HEADS * HEAD_DIM)
        grad_sum = jnp.zeros((LEN, D), jnp.float32)
        key_down_total, value_down_total, key_up_total, value_up_total = state_sum
        for shard_index in range(N_MP):
            key_start = shard_index * key_width
            key_stop = key_start + key_width
            query_start = shard_index * query_width
            query_stop = query_start + query_width
            key_coefficient = final_product(key_adapter_change[:, key_start:key_stop], key_up_matrix[:, key_start:key_stop]).astype(jnp.bfloat16)
            value_coefficient = final_product(value_adapter_change[:, key_start:key_stop], value_up_matrix[:, key_start:key_stop]).astype(jnp.bfloat16)
            portion_total = final_product(key_adapter_change[:, key_start:key_stop], key_weight_matrix[:, key_start:key_stop]) + final_product(value_adapter_change[:, key_start:key_stop], value_weight_matrix[:, key_start:key_stop])
            portion_total = portion_total + ADAPTER_SCALE * (final_product(key_coefficient.astype(jnp.float32), key_down_float) + final_product(value_coefficient.astype(jnp.float32), value_down_float))
            last_part = final_product(query_delta[:, query_start:query_stop], w_query[:, query_start:query_stop])
            portion_total = portion_total.at[length - 1].add(last_part[0])
            grad_sum = grad_sum + rounded(portion_total)
            key_down_total = key_down_total + ADAPTER_SCALE * first_product(token_inputs, key_coefficient)
            value_down_total = value_down_total + ADAPTER_SCALE * first_product(token_inputs, value_coefficient)
        grad_sum = grad_sum.at[length - 1].add(cotangent.astype(jnp.float32))
        key_up_total = key_up_total + ADAPTER_SCALE * first_product(reduced_key, key_adapter_change)
        value_up_total = value_up_total + ADAPTER_SCALE * first_product(reduced_value, value_adapter_change)
        return ((key_down_total, value_down_total, key_up_total, value_up_total), grad_sum.astype(jnp.bfloat16))
    start_state = (jnp.zeros((D, RANK), jnp.float32), jnp.zeros((D, RANK), jnp.float32), jnp.zeros((RANK, KV_HEADS * HEAD_DIM), jnp.float32), jnp.zeros((RANK, KV_HEADS * HEAD_DIM), jnp.float32))
    final_state, grad_rows = lax.scan(one_sequence, start_state, (flat_x, flat_len, cotangents))
    input_grad = grad_rows.reshape(SUBS, SEQS, LEN, D)
    return (mean_loss, query_grad, item_grad, input_grad, final_state[0], final_state[1], final_state[2], final_state[3])
```

```python
import functools
import math

import jax
import jax.numpy as jnp
from jax import lax
from jax.experimental import pallas as pl
from jax.experimental.pallas import tpu as pltpu
from jax.sharding import PartitionSpec as P

HEADS = 32
KV_HEADS = 8
HEAD_DIM = 128


INV_TEMP = 50.0
HARD_NEGATIVE_ADD = 4.0
ADAPTER_SCALE = 2.0


def final_product(left_side, right_side):
    return lax.dot_general(
        left_side, right_side, (((1,), (1,)), ((), ())), preferred_element_type=jnp.float32
    )


def first_product(left_side, right_side):
    return lax.dot_general(
        left_side, right_side, (((0,), (0,)), ((), ())), preferred_element_type=jnp.float32
    )


def local(
    query_emb,
    item_emb,
    pair_index,
    hard_index,
    hidden_in,
    lengths,
    w_query,
    key_weight_matrix,
    value_weight_matrix,
    w_out,
    key_down_matrix,
    key_up_matrix,
    value_down,
    value_up_matrix,
):
    dp_count = lax.axis_size("dp")
    local_rows = query_emb.shape[0]
    batch_size = local_rows * dp_count
    items_all = lax.all_gather(item_emb, "dp", axis=0, tiled=True)
    partial_scores = final_product(query_emb, items_all)
    pair_scores = lax.psum(partial_scores, "mp") * INV_TEMP
    columns = jnp.arange(batch_size, dtype=jnp.int32)
    hard_negative_count = jnp.sum(
        (hard_index[:, :, None] == columns[None, None, :]).astype(jnp.float32), axis=1
    )
    score_logits = pair_scores + HARD_NEGATIVE_ADD * hard_negative_count
    row_top = jnp.max(score_logits, axis=1, keepdims=True)
    log_total = row_top[:, 0] + jnp.log(jnp.sum(jnp.exp(score_logits - row_top), axis=1))
    target = (pair_index[:, None] == columns[None, :]).astype(jnp.float32)
    picked = jnp.sum(target * score_logits, axis=1)
    loss_part = jnp.sum(log_total - picked)
    residual = (jnp.exp(score_logits - log_total[:, None]) - target).astype(jnp.bfloat16)
    query_grad = (
        jnp.dot(residual, items_all, preferred_element_type=jnp.float32) * INV_TEMP
    ).astype(jnp.bfloat16)
    item_grad = lax.psum_scatter(
        first_product(residual, query_emb) * INV_TEMP, "dp", scatter_dimension=0, tiled=True
    ).astype(jnp.bfloat16)
    sub_count = hidden_in.shape[0]
    seq_len = hidden_in.shape[2]
    full_rows = lax.all_gather(hidden_in, "mp", axis=3, tiled=True)
    model_width = full_rows.shape[3]
    token_inputs = full_rows.reshape(sub_count * seq_len, model_width)
    seq_lengths = lengths[:, 0]
    last_rows = jnp.arange(sub_count, dtype=jnp.int32) * seq_len + seq_lengths - 1
    last_tokens = jnp.take(token_inputs, last_rows, axis=0)
    cot_local = item_grad[:sub_count]
    cot_full = lax.all_gather(cot_local, "mp", axis=1, tiled=True)
    adapter_rank = key_down_matrix.shape[1]
    down_both = jnp.concatenate([key_down_matrix, value_down], axis=1)
    reduced_pair = jnp.dot(token_inputs, down_both, preferred_element_type=jnp.float32).astype(
        jnp.bfloat16
    )
    reduced_key = reduced_pair[:, :adapter_rank]
    reduced_value = reduced_pair[:, adapter_rank:]
    key_rows = (
        jnp.dot(token_inputs, key_weight_matrix, preferred_element_type=jnp.float32)
        + ADAPTER_SCALE * jnp.dot(reduced_key, key_up_matrix, preferred_element_type=jnp.float32)
    ).astype(jnp.bfloat16)
    value_rows = (
        jnp.dot(token_inputs, value_weight_matrix, preferred_element_type=jnp.float32)
        + ADAPTER_SCALE
        * jnp.dot(reduced_value, value_up_matrix, preferred_element_type=jnp.float32)
    ).astype(jnp.bfloat16)
    query_width = w_query.shape[1]
    wq_full, wo_full = (
        lax.all_gather(w_query, "dp", axis=0, tiled=True),
        lax.all_gather(w_out, "dp", axis=1, tiled=True),
    )
    query = jnp.dot(last_tokens, wq_full, preferred_element_type=jnp.float32).astype(jnp.bfloat16)
    attn_grad = final_product(cot_full, wo_full).astype(jnp.bfloat16)
    group_size = HEADS // KV_HEADS
    kv_local = key_rows.shape[1] // HEAD_DIM
    score_scale = 1.0 / math.sqrt(HEAD_DIM)
    q_heads = query.reshape(sub_count, kv_local, group_size, HEAD_DIM)
    k_heads = key_rows.reshape(sub_count, seq_len, kv_local, HEAD_DIM)
    v_heads = value_rows.reshape(sub_count, seq_len, kv_local, HEAD_DIM)
    raw_scores = (
        jnp.einsum("bkgd,bjkd->bkgj", q_heads, k_heads, preferred_element_type=jnp.float32)
        * score_scale
    )
    live_mask = jnp.arange(seq_len, dtype=jnp.int32)[None, :] < seq_lengths[:, None]
    raw_scores = jnp.where(live_mask[:, None, None, :], raw_scores, -jnp.inf)
    row_peak = jnp.max(raw_scores, axis=-1, keepdims=True)
    weights = jnp.exp(raw_scores - row_peak)
    softmax_probs = weights / jnp.sum(weights, axis=-1, keepdims=True)
    prob_half = softmax_probs.astype(jnp.bfloat16)
    grad_heads = attn_grad.reshape(sub_count, kv_local, group_size, HEAD_DIM)
    prob_grad = jnp.einsum(
        "bkgd,bjkd->bkgj", grad_heads, v_heads, preferred_element_type=jnp.float32
    )
    score_grad = (
        softmax_probs
        * (prob_grad - jnp.sum(softmax_probs * prob_grad, axis=-1, keepdims=True))
        * score_scale
    ).astype(jnp.bfloat16)
    query_delta = (
        jnp.einsum("bkgj,bjkd->bkgd", score_grad, k_heads, preferred_element_type=jnp.float32)
        .astype(jnp.bfloat16)
        .reshape(sub_count, query_width)
    )
    key_adapter_change = (
        jnp.einsum("bkgj,bkgd->bjkd", score_grad, q_heads, preferred_element_type=jnp.float32)
        .astype(jnp.bfloat16)
        .reshape(sub_count * seq_len, kv_local * HEAD_DIM)
    )
    value_adapter_change = (
        jnp.einsum("bkgj,bkgd->bjkd", prob_half, grad_heads, preferred_element_type=jnp.float32)
        .astype(jnp.bfloat16)
        .reshape(sub_count * seq_len, kv_local * HEAD_DIM)
    )
    last_part = final_product(query_delta, wq_full)
    key_coefficient = final_product(key_adapter_change, key_up_matrix).astype(jnp.bfloat16)
    value_coefficient = final_product(value_adapter_change, value_up_matrix).astype(jnp.bfloat16)
    input_portion = final_product(key_adapter_change, key_weight_matrix) + final_product(
        value_adapter_change, value_weight_matrix
    )
    input_portion = input_portion + ADAPTER_SCALE * (
        final_product(key_coefficient, key_down_matrix)
        + final_product(value_coefficient, value_down)
    )
    input_portion = input_portion.at[last_rows].add(last_part)
    input_sum = lax.psum_scatter(
        input_portion.astype(jnp.bfloat16), "mp", scatter_dimension=1, tiled=True
    ).astype(jnp.float32)
    input_sum = input_sum.at[last_rows].add(cot_local.astype(jnp.float32))
    input_grad = input_sum.astype(jnp.bfloat16).reshape(hidden_in.shape)
    key_down_grad, value_down_grad = lax.psum(
        (
            ADAPTER_SCALE * first_product(token_inputs, key_coefficient),
            ADAPTER_SCALE * first_product(token_inputs, value_coefficient),
        ),
        ("dp", "mp"),
    )
    total_loss, key_up_grad, value_up_grad = lax.psum(
        (
            loss_part,
            ADAPTER_SCALE * first_product(reduced_key, key_adapter_change),
            ADAPTER_SCALE * first_product(reduced_value, value_adapter_change),
        ),
        "dp",
    )
    mean_loss = total_loss / batch_size
    return (
        mean_loss,
        query_grad,
        item_grad,
        input_grad,
        key_down_grad,
        value_down_grad,
        key_up_grad,
        value_up_grad,
    )


TILE = 512
EMB, IDX, XS, QP, CS, AP, QD, LP, DN, UP, DNG, UPG = range(12)
M_XL, M_X, M_SC, M_COT, M_COEF, M_PART, M_LAST, M_DN = range(8)


def plain_product(left_side, right_side):
    return jnp.dot(left_side, right_side, preferred_element_type=jnp.float32)


def step_kernel(
    dp, mp, subs, rank,
    len_ref, emb_ref, idx_ref, x_hbm, wq_hbm, wk_hbm, wv_hbm, wo_hbm, down_ref, kup_ref, vup_ref,
    loss_ref, emb_grad_ref, input_grad_ref, down_out, up_out,
    emb_all, idx_all, xg, xl_g, xs, xr, x_rows, part_q, land_q, cot_g, cs, cr, cot_rows,
    part_a, land_a, scores_g, sym, wq, wk, wv, wo, acc_k, acc_v, acc_low, q_blk, g_blk,
    query_f, grad_f, qd_own, qd_all, qd_rows, lp, lp_land, coef_g, pacc, pbuf, pland, last_rows_f,
    last_send, last_land, dn, dn_land, up, up_land, last_total, ssem, rsem, msend, mrecv, csem,
):
    me = lax.axis_index("dp")
    core = lax.axis_index("mp")
    other = 1 - core
    rows, feats = x_hbm.shape
    seq_len = rows // subs
    group_rows = emb_ref.shape[0]
    half_rows = group_rows // 2
    total_rows = dp * group_rows
    dq, qw = wq.shape
    kw = wk.shape[1]
    tiles = feats // TILE

    local_copies = [
        pltpu.make_async_copy(src, dst, csem.at[i])
        for i, (src, dst) in enumerate(
            ((x_hbm, xg.at[core]), (wq_hbm, wq), (wk_hbm, wk), (wv_hbm, wv), (wo_hbm, wo))
        )
    ]
    for copy in local_copies:
        copy.start()

    barrier = pltpu.get_barrier_semaphore()

    @pl.loop(1, dp)
    def _(k):
        pl.semaphore_signal(
            barrier, inc=1, device_id=(lax.rem(me + k, dp), core), device_id_type=pl.DeviceIdType.MESH
        )

    pl.semaphore_signal(barrier, inc=1, device_id=(me, other), device_id_type=pl.DeviceIdType.MESH)
    pl.semaphore_wait(barrier, dp)

    def dp_copy(op, k, source, landing):
        target = lax.rem(me + k, dp)
        return pltpu.make_async_remote_copy(
            src_ref=source(target),
            dst_ref=landing.at[me],
            send_sem=ssem.at[op, k],
            recv_sem=rsem.at[op, k],
            device_id=(target, core),
            device_id_type=pl.DeviceIdType.MESH,
        )

    def dp_start(op, source, landing):
        @pl.loop(1, dp)
        def _(k):
            dp_copy(op, k, source, landing).start()

    def dp_wait(op, source, landing):
        @pl.loop(1, dp)
        def _(k):
            dp_copy(op, k, source, landing).wait()

    def mp_copy(op, source, landing):
        return pltpu.make_async_remote_copy(
            src_ref=source,
            dst_ref=landing,
            send_sem=msend.at[op],
            recv_sem=mrecv.at[op],
            device_id=(me, other),
            device_id_type=pl.DeviceIdType.MESH,
        )

    emb_args = (EMB, lambda t: emb_ref, emb_all)
    idx_args = (IDX, lambda t: idx_ref, idx_all)
    dp_start(*emb_args)
    dp_start(*idx_args)
    emb_all[me] = emb_ref[...]
    idx_all[me] = idx_ref[...]

    local_copies[0].wait()
    last = [jnp.clip(len_ref[b] - 1, 0, seq_len - 1) + b * seq_len for b in range(subs)]
    one_row = lax.broadcasted_iota(jnp.int32, (8, rows), 0)
    one_col = lax.broadcasted_iota(jnp.int32, (8, rows), 1)
    picked_rows = jnp.zeros((8, rows), jnp.float32)
    for b in range(subs):
        picked_rows = jnp.where((one_row == b) & (one_col == last[b]), 1.0, picked_rows)
    xl_g[core] = plain_product(picked_rows.astype(jnp.bfloat16), xg[core])[:subs]
    xl_copy = mp_copy(M_XL, xl_g.at[core], xl_g.at[core])
    xl_copy.start()
    x_copy = mp_copy(M_X, xg.at[core], xg.at[core])
    x_copy.start()
    xl_copy.wait()
    per_core = dp // mp
    for j in range(dp):
        start = (j % per_core) * dq
        xs[j] = xl_g[j // per_core, :, start : start + dq]
    xs_args = (XS, lambda t: xs.at[t], xr)
    dp_start(*xs_args)
    xr[me] = xs[me]

    dp_wait(*emb_args)
    dp_wait(*idx_args)
    emb_rows = emb_all[...].reshape(total_rows, feats)
    scores_g[core] = final_product(emb_rows, emb_rows)
    score_copy = mp_copy(M_SC, scores_g.at[core], scores_g.at[core])
    score_copy.start()

    dp_wait(*xs_args)
    for j in range(dp):
        x_rows[j * subs : (j + 1) * subs, :] = xr[j]
    local_copies[1].wait()
    query_part = plain_product(x_rows[...].astype(jnp.bfloat16), wq[...])
    for j in range(dp):
        part_q[j] = query_part[j * subs : (j + 1) * subs]
    q_args = (QP, lambda t: part_q.at[t], land_q)
    dp_start(*q_args)
    land_q[me] = part_q[me]

    score_copy.wait()
    logits = (scores_g[0] + scores_g[1]) * INV_TEMP
    columns = lax.broadcasted_iota(jnp.int32, (total_rows, total_rows), 1)
    row_ids = lax.broadcasted_iota(jnp.int32, (total_rows, total_rows), 0)
    index_rows = idx_all[...].reshape(total_rows, idx_ref.shape[1])
    hard_count = jnp.zeros((total_rows, total_rows), jnp.float32)
    for h in range(4):
        hard_count = hard_count + jnp.where(columns == index_rows[:, h + 1 : h + 2], 1.0, 0.0)
    logits = logits + HARD_NEGATIVE_ADD * hard_count
    is_item = lax.rem(columns, group_rows) >= half_rows
    is_query = lax.rem(row_ids, group_rows) < half_rows
    live_logits = jnp.where(is_item, logits, -jnp.inf)
    row_top = jnp.max(live_logits, axis=1, keepdims=True)
    log_total = row_top + jnp.log(jnp.sum(jnp.exp(live_logits - row_top), axis=1, keepdims=True))
    target = jnp.where(columns == index_rows[:, 0:1], 1.0, 0.0)
    picked = jnp.sum(target * logits, axis=1, keepdims=True)
    loss_rows = jnp.where(is_query[:, 0:1], log_total - picked, 0.0)
    loss_total = jnp.sum(loss_rows, axis=0, keepdims=True) / (total_rows // 2)
    loss_ref[...] = jnp.broadcast_to(loss_total, loss_ref.shape)
    residual = jnp.where(is_query, jnp.exp(live_logits - log_total) - target, 0.0)
    residual = residual.astype(jnp.bfloat16).astype(jnp.float32)
    sym[...] = (residual + residual.T).astype(jnp.bfloat16).reshape(dp, group_rows, total_rows)
    own_grad = (plain_product(sym[me], emb_rows) * INV_TEMP).astype(jnp.bfloat16)
    emb_grad_ref[...] = own_grad
    cot_g[core] = own_grad.astype(jnp.float32)[half_rows : half_rows + subs]
    cot_copy = mp_copy(M_COT, cot_g.at[core], cot_g.at[core])
    cot_copy.start()
    cot_copy.wait()
    for j in range(dp):
        start = (j % per_core) * dq
        cs[j] = cot_g[j // per_core, :, start : start + dq]
    cs_args = (CS, lambda t: cs.at[t], cr)
    dp_start(*cs_args)
    cr[me] = cs[me]

    acc_k[...] = jnp.zeros_like(acc_k)
    acc_v[...] = jnp.zeros_like(acc_v)
    acc_low[...] = jnp.zeros_like(acc_low)
    local_copies[2].wait()
    local_copies[3].wait()

    def project(which):
        @pl.loop(0, tiles)
        def _(t):
            cols = pl.ds(pl.multiple_of(t * TILE, TILE), TILE)
            spot = pl.ds(pl.multiple_of(which * feats + t * TILE, TILE), TILE)
            block = xg[which, :, cols]
            acc_k[...] += plain_product(block, wk[spot, :])
            acc_v[...] += plain_product(block, wv[spot, :])
            acc_low[...] += final_product(block, down_ref[:, spot])

    project(core)

    dp_wait(*cs_args)
    for j in range(dp):
        cot_rows[j * subs : (j + 1) * subs, :] = cr[j]
    local_copies[4].wait()
    grad_part = final_product(cot_rows[...].astype(jnp.bfloat16), wo[...])
    for j in range(dp):
        part_a[j] = grad_part[j * subs : (j + 1) * subs]
    a_args = (AP, lambda t: part_a.at[t], land_a)
    dp_start(*a_args)
    land_a[me] = part_a[me]

    x_copy.wait()
    project(other)
    low = acc_low[...].astype(jnp.bfloat16)
    low_key, low_value = low[:, :rank], low[:, rank:]
    keys = (acc_k[...] + ADAPTER_SCALE * plain_product(low_key, kup_ref[...])).astype(jnp.bfloat16)
    values = (acc_v[...] + ADAPTER_SCALE * plain_product(low_value, vup_ref[...])).astype(
        jnp.bfloat16
    )

    heads = qw // HEAD_DIM
    group_size = HEADS // KV_HEADS
    score_scale = 1.0 / math.sqrt(HEAD_DIM)

    def spread(flat, blocks):
        blocks[...] = jnp.zeros_like(blocks)
        for b in range(subs):
            for h in range(heads):
                kv = h // group_size * HEAD_DIM
                blocks[b * heads + h : b * heads + h + 1, kv : kv + HEAD_DIM] = flat[
                    b : b + 1, h * HEAD_DIM : (h + 1) * HEAD_DIM
                ]

    def summed(landing):
        total = landing[0]
        for j in range(1, dp):
            total = total + landing[j]
        return total.astype(jnp.bfloat16).astype(jnp.float32)

    dp_wait(*q_args)
    query_f[...] = summed(land_q)
    spread(query_f, q_blk)
    q_half = q_blk[...].astype(jnp.bfloat16)
    raw = final_product(q_half, keys) * score_scale
    head_rows = lax.broadcasted_iota(jnp.int32, raw.shape, 0)
    token_ids = lax.broadcasted_iota(jnp.int32, raw.shape, 1)
    live = jnp.zeros(raw.shape, jnp.bool_)
    for b in range(subs):
        mine = (head_rows >= b * heads) & (head_rows < (b + 1) * heads)
        live = live | (mine & (token_ids >= b * seq_len) & (token_ids <= last[b]))
    raw = jnp.where(live, raw, -jnp.inf)
    weights = jnp.exp(raw - jnp.max(raw, axis=1, keepdims=True))
    probs = weights / jnp.sum(weights, axis=1, keepdims=True)
    dp_wait(*a_args)
    grad_f[...] = summed(land_a)
    spread(grad_f, g_blk)
    g_half = g_blk[...].astype(jnp.bfloat16)
    prob_grad = final_product(g_half, values)
    score_grad = (
        probs * (prob_grad - jnp.sum(probs * prob_grad, axis=1, keepdims=True)) * score_scale
    ).astype(jnp.bfloat16)
    query_delta = plain_product(score_grad, keys).astype(jnp.bfloat16).astype(jnp.float32)
    for b in range(subs):
        for h in range(heads):
            kv = h // group_size * HEAD_DIM
            qd_own[b : b + 1, h * HEAD_DIM : (h + 1) * HEAD_DIM] = query_delta[
                b * heads + h : b * heads + h + 1, kv : kv + HEAD_DIM
            ]
    qd_args = (QD, lambda t: qd_own, qd_all)
    dp_start(*qd_args)
    qd_all[me] = qd_own[...]
    key_delta = first_product(score_grad, q_half).astype(jnp.bfloat16)
    value_delta = first_product(probs.astype(jnp.bfloat16), g_half).astype(jnp.bfloat16)
    coef = jnp.concatenate(
        [final_product(key_delta, kup_ref[...]), final_product(value_delta, vup_ref[...])], axis=1
    ).astype(jnp.bfloat16)
    coef_g[core] = coef
    coef_copy = mp_copy(M_COEF, coef_g.at[core], coef_g.at[core])
    coef_copy.start()

    key_up = ADAPTER_SCALE * first_product(low_key, key_delta)
    value_up = ADAPTER_SCALE * first_product(low_value, value_delta)
    up_rows = 2 * rank // dp
    for j in range(dp):
        spot = j * up_rows
        up[j] = key_up[spot : spot + up_rows] if spot < rank else value_up[
            spot - rank : spot - rank + up_rows
        ]
    up_args = (UP, lambda t: up.at[t], up_land)
    dp_start(*up_args)
    up_land[me] = up[me]

    coef_copy.wait()
    down_part = ADAPTER_SCALE * (
        first_product(coef_g[0], xg[core]) + first_product(coef_g[1], xg[core])
    )
    down_cols = feats // dp
    for j in range(dp):
        dn[j] = down_part[:, j * down_cols : (j + 1) * down_cols]
    dn_args = (DN, lambda t: dn.at[t], dn_land)
    dp_start(*dn_args)
    dn_land[me] = dn[me]

    dp_wait(*qd_args)
    for j in range(dp):
        qd_rows[j * subs : (j + 1) * subs, :] = qd_all[j]
    last_part = final_product(qd_rows[...].astype(jnp.bfloat16), wq[...])
    for j in range(dp):
        lp[j] = last_part[j * subs : (j + 1) * subs]
    lp_args = (LP, lambda t: lp.at[t], lp_land)
    dp_start(*lp_args)
    lp_land[me] = lp[me]

    def portion(which, slot):
        @pl.loop(0, tiles)
        def _(t):
            cols = pl.ds(pl.multiple_of(t * TILE, TILE), TILE)
            spot = pl.ds(pl.multiple_of(which * feats + t * TILE, TILE), TILE)
            pacc[...] = (
                final_product(key_delta, wk[spot, :])
                + final_product(value_delta, wv[spot, :])
                + ADAPTER_SCALE * plain_product(coef, down_ref[:, spot])
            )
            pbuf[slot, :, cols] = pacc[...].astype(jnp.bfloat16)
            for b in range(subs):
                last_rows_f[slot, b : b + 1, cols] = pacc[pl.ds(last[b], 1), :]

    portion(other, 1)
    part_copy = mp_copy(M_PART, pbuf.at[1], pland)
    part_copy.start()

    dp_wait(*dn_args)
    total = dn_land[0]
    for j in range(1, dp):
        total = total + dn_land[j]
    down_out[core, me] = total
    dng_args = (DNG, lambda t: down_out.at[core, me], down_out.at[core])
    dp_start(*dng_args)
    dp_wait(*up_args)
    total = up_land[0]
    for j in range(1, dp):
        total = total + up_land[j]
    up_out[me] = total
    upg_args = (UPG, lambda t: up_out.at[me], up_out)
    dp_start(*upg_args)

    portion(core, 0)

    dp_wait(*lp_args)
    for which in range(mp):
        for j in range(per_core):
            last_total[which, :, j * dq : (j + 1) * dq] = lp_land[which * per_core + j]
    last_send[...] = (
        (last_rows_f[1] + last_total[other]).astype(jnp.bfloat16).astype(jnp.float32)
    )
    last_copy = mp_copy(M_LAST, last_send, last_land)
    last_copy.start()
    dp_wait(*dng_args)
    down_copy = mp_copy(M_DN, down_out.at[core], down_out.at[core])
    down_copy.start()

    own_last = (last_rows_f[0] + last_total[core]).astype(jnp.bfloat16).astype(jnp.float32)
    last_copy.wait()
    last_rows_f[0] = own_last + last_land[...] + cot_g[core]
    part_copy.wait()

    @pl.loop(0, tiles)
    def _(t):
        cols = pl.ds(pl.multiple_of(t * TILE, TILE), TILE)
        both = pbuf[0, :, cols].astype(jnp.float32) + pland[:, cols].astype(jnp.float32)
        ids = lax.broadcasted_iota(jnp.int32, both.shape, 0)
        for b in range(subs):
            both = jnp.where(ids == last[b], last_rows_f[0, b : b + 1, cols], both)
        input_grad_ref[:, cols] = both.astype(jnp.bfloat16)

    dp_wait(*upg_args)
    down_copy.wait()


def fused_local(
    query_emb, item_emb, pair_index, hard_index, hidden_in, lengths, w_query, key_weight_matrix,
    value_weight_matrix, w_out, key_down_matrix, key_up_matrix, value_down, value_up_matrix,
):
    dp, mp = lax.axis_size("dp"), lax.axis_size("mp")
    local_rows, feats = query_emb.shape
    subs, _, seq_len, _ = hidden_in.shape
    rows = subs * seq_len
    rank, kw = key_up_matrix.shape
    dq, qw = w_query.shape
    width = feats * mp
    heads = qw // HEAD_DIM
    group_rows = 2 * local_rows
    total_rows = dp * group_rows
    emb = jnp.concatenate([query_emb, item_emb], axis=0)
    index = jnp.concatenate([pair_index[:, None], hard_index], axis=1)
    index = index // local_rows * group_rows + local_rows + index % local_rows
    index = jnp.pad(index, ((0, local_rows), (0, 128 - index.shape[1])), constant_values=-1)
    down = jnp.concatenate([key_down_matrix.T, value_down.T], axis=0)
    f32, bf16 = jnp.float32, jnp.bfloat16
    vmem, hbm = pl.BlockSpec(memory_space=pltpu.VMEM), pl.BlockSpec(memory_space=pl.ANY)
    shape = jax.ShapeDtypeStruct
    scratch = [
        ((dp, group_rows, feats), bf16),
        ((dp, group_rows, 128), jnp.int32),
        ((mp, rows, feats), bf16),
        ((mp, subs, feats), f32),
        ((dp, subs, dq), f32),
        ((dp, subs, dq), f32),
        ((dp * subs, dq), f32),
        ((dp, subs, qw), f32),
        ((dp, subs, qw), f32),
        ((mp, subs, feats), f32),
        ((dp, subs, dq), f32),
        ((dp, subs, dq), f32),
        ((dp * subs, dq), f32),
        ((dp, subs, qw), f32),
        ((dp, subs, qw), f32),
        ((mp, total_rows, total_rows), f32),
        ((dp, group_rows, total_rows), bf16),
        ((dq, qw), bf16),
        ((width, kw), bf16),
        ((width, kw), bf16),
        ((qw, dq), bf16),
        ((rows, kw), f32),
        ((rows, kw), f32),
        ((rows, 2 * rank), f32),
        ((subs * heads, kw), f32),
        ((subs * heads, kw), f32),
        ((subs, qw), f32),
        ((subs, qw), f32),
        ((subs, qw), f32),
        ((dp, subs, qw), f32),
        ((dp * subs, qw), f32),
        ((dp, subs, dq), f32),
        ((dp, subs, dq), f32),
        ((mp, rows, 2 * rank), bf16),
        ((rows, TILE), f32),
        ((2, rows, feats), bf16),
        ((rows, feats), bf16),
        ((2, subs, feats), f32),
        ((subs, feats), f32),
        ((subs, feats), f32),
        ((dp, 2 * rank, feats // dp), f32),
        ((dp, 2 * rank, feats // dp), f32),
        ((dp, 2 * rank // dp, kw), f32),
        ((dp, 2 * rank // dp, kw), f32),
        ((mp, subs, feats), f32),
    ]
    loss, emb_grad, input_grad, down_grad, up_grad = pl.pallas_call(
        functools.partial(step_kernel, dp, mp, subs, rank),
        out_shape=(
            shape((8, 128), f32),
            shape((group_rows, feats), bf16),
            shape((rows, feats), bf16),
            shape((mp, dp, 2 * rank, feats // dp), f32),
            shape((dp, 2 * rank // dp, kw), f32),
        ),
        in_specs=[pl.BlockSpec(memory_space=pltpu.SMEM), vmem, vmem]
        + [hbm] * 5
        + [vmem] * 3,
        out_specs=(vmem,) * 5,
        scratch_shapes=[pltpu.VMEM(s, t) for s, t in scratch]
        + [
            pltpu.SemaphoreType.DMA((12, dp)),
            pltpu.SemaphoreType.DMA((12, dp)),
            pltpu.SemaphoreType.DMA((8,)),
            pltpu.SemaphoreType.DMA((8,)),
            pltpu.SemaphoreType.DMA((5,)),
        ],
        compiler_params=pltpu.CompilerParams(
            collective_id=0, has_side_effects=True, vmem_limit_bytes=60 * 1024 * 1024
        ),
    )(
        lengths[:, 0], emb, index, hidden_in.reshape(rows, feats), w_query, key_weight_matrix,
        value_weight_matrix, w_out, down, key_up_matrix, value_up_matrix,
    )
    down_grad = down_grad.transpose(2, 0, 1, 3).reshape(2 * rank, width)
    up_grad = up_grad.reshape(2 * rank, kw)
    return (
        loss[0, 0],
        emb_grad[:local_rows],
        emb_grad[local_rows:],
        input_grad.reshape(hidden_in.shape),
        down_grad[:rank].T,
        down_grad[rank:].T,
        up_grad[:rank],
        up_grad[rank:],
    )


def solution(mesh):
    in_specs = (
        P("dp", "mp"),
        P("dp", "mp"),
        P("dp"),
        P("dp", None),
        P(None, "dp", None, "mp"),
        P(None, "dp"),
        P("dp", "mp"),
        P(None, "mp"),
        P(None, "mp"),
        P("mp", "dp"),
        P(),
        P(None, "mp"),
        P(),
        P(None, "mp"),
    )
    out_specs = (
        P(),
        P("dp", "mp"),
        P("dp", "mp"),
        P(None, "dp", None, "mp"),
        P(),
        P(),
        P(None, "mp"),
        P(None, "mp"),
    )
    small = mesh.shape["mp"] == 2 and mesh.shape["dp"] == 16
    body = fused_local if small else local
    return jax.shard_map(body, mesh=mesh, in_specs=in_specs, out_specs=out_specs, check_vma=False)
```

```python
import functools
import math

import jax
import jax.numpy as jnp
from jax import lax
from jax.experimental import pallas as pl
from jax.experimental.pallas import tpu as pltpu
from jax.sharding import PartitionSpec as P

HEADS = 32
KV_HEADS = 8
HEAD_DIM = 128


INV_TEMP = 50.0
HARD_NEGATIVE_ADD = 4.0
ADAPTER_SCALE = 2.0


def final_product(left_side, right_side):
    return lax.dot_general(
        left_side, right_side, (((1,), (1,)), ((), ())), preferred_element_type=jnp.float32
    )


def first_product(left_side, right_side):
    return lax.dot_general(
        left_side, right_side, (((0,), (0,)), ((), ())), preferred_element_type=jnp.float32
    )


def local(
    query_emb,
    item_emb,
    pair_index,
    hard_index,
    hidden_in,
    lengths,
    w_query,
    key_weight_matrix,
    value_weight_matrix,
    w_out,
    key_down_matrix,
    key_up_matrix,
    value_down,
    value_up_matrix,
):
    dp_count = lax.axis_size("dp")
    local_rows = query_emb.shape[0]
    batch_size = local_rows * dp_count
    items_all = lax.all_gather(item_emb, "dp", axis=0, tiled=True)
    partial_scores = final_product(query_emb, items_all)
    pair_scores = lax.psum(partial_scores, "mp") * INV_TEMP
    columns = jnp.arange(batch_size, dtype=jnp.int32)
    hard_negative_count = jnp.sum(
        (hard_index[:, :, None] == columns[None, None, :]).astype(jnp.float32), axis=1
    )
    score_logits = pair_scores + HARD_NEGATIVE_ADD * hard_negative_count
    row_top = jnp.max(score_logits, axis=1, keepdims=True)
    log_total = row_top[:, 0] + jnp.log(jnp.sum(jnp.exp(score_logits - row_top), axis=1))
    target = (pair_index[:, None] == columns[None, :]).astype(jnp.float32)
    picked = jnp.sum(target * score_logits, axis=1)
    loss_part = jnp.sum(log_total - picked)
    residual = (jnp.exp(score_logits - log_total[:, None]) - target).astype(jnp.bfloat16)
    query_grad = (
        jnp.dot(residual, items_all, preferred_element_type=jnp.float32) * INV_TEMP
    ).astype(jnp.bfloat16)
    item_grad = lax.psum_scatter(
        first_product(residual, query_emb) * INV_TEMP, "dp", scatter_dimension=0, tiled=True
    ).astype(jnp.bfloat16)
    sub_count = hidden_in.shape[0]
    seq_len = hidden_in.shape[2]
    full_rows = lax.all_gather(hidden_in, "mp", axis=3, tiled=True)
    model_width = full_rows.shape[3]
    token_inputs = full_rows.reshape(sub_count * seq_len, model_width)
    seq_lengths = lengths[:, 0]
    last_rows = jnp.arange(sub_count, dtype=jnp.int32) * seq_len + seq_lengths - 1
    last_tokens = jnp.take(token_inputs, last_rows, axis=0)
    cot_local = item_grad[:sub_count]
    cot_full = lax.all_gather(cot_local, "mp", axis=1, tiled=True)
    adapter_rank = key_down_matrix.shape[1]
    down_both = jnp.concatenate([key_down_matrix, value_down], axis=1)
    reduced_pair = jnp.dot(token_inputs, down_both, preferred_element_type=jnp.float32).astype(
        jnp.bfloat16
    )
    reduced_key = reduced_pair[:, :adapter_rank]
    reduced_value = reduced_pair[:, adapter_rank:]
    key_rows = (
        jnp.dot(token_inputs, key_weight_matrix, preferred_element_type=jnp.float32)
        + ADAPTER_SCALE * jnp.dot(reduced_key, key_up_matrix, preferred_element_type=jnp.float32)
    ).astype(jnp.bfloat16)
    value_rows = (
        jnp.dot(token_inputs, value_weight_matrix, preferred_element_type=jnp.float32)
        + ADAPTER_SCALE
        * jnp.dot(reduced_value, value_up_matrix, preferred_element_type=jnp.float32)
    ).astype(jnp.bfloat16)
    query_width = w_query.shape[1]
    wq_full, wo_full = (
        lax.all_gather(w_query, "dp", axis=0, tiled=True),
        lax.all_gather(w_out, "dp", axis=1, tiled=True),
    )
    query = jnp.dot(last_tokens, wq_full, preferred_element_type=jnp.float32).astype(jnp.bfloat16)
    attn_grad = final_product(cot_full, wo_full).astype(jnp.bfloat16)
    group_size = HEADS // KV_HEADS
    kv_local = key_rows.shape[1] // HEAD_DIM
    score_scale = 1.0 / math.sqrt(HEAD_DIM)
    q_heads = query.reshape(sub_count, kv_local, group_size, HEAD_DIM)
    k_heads = key_rows.reshape(sub_count, seq_len, kv_local, HEAD_DIM)
    v_heads = value_rows.reshape(sub_count, seq_len, kv_local, HEAD_DIM)
    raw_scores = (
        jnp.einsum("bkgd,bjkd->bkgj", q_heads, k_heads, preferred_element_type=jnp.float32)
        * score_scale
    )
    live_mask = jnp.arange(seq_len, dtype=jnp.int32)[None, :] < seq_lengths[:, None]
    raw_scores = jnp.where(live_mask[:, None, None, :], raw_scores, -jnp.inf)
    row_peak = jnp.max(raw_scores, axis=-1, keepdims=True)
    weights = jnp.exp(raw_scores - row_peak)
    softmax_probs = weights / jnp.sum(weights, axis=-1, keepdims=True)
    prob_half = softmax_probs.astype(jnp.bfloat16)
    grad_heads = attn_grad.reshape(sub_count, kv_local, group_size, HEAD_DIM)
    prob_grad = jnp.einsum(
        "bkgd,bjkd->bkgj", grad_heads, v_heads, preferred_element_type=jnp.float32
    )
    score_grad = (
        softmax_probs
        * (prob_grad - jnp.sum(softmax_probs * prob_grad, axis=-1, keepdims=True))
        * score_scale
    ).astype(jnp.bfloat16)
    query_delta = (
        jnp.einsum("bkgj,bjkd->bkgd", score_grad, k_heads, preferred_element_type=jnp.float32)
        .astype(jnp.bfloat16)
        .reshape(sub_count, query_width)
    )
    key_adapter_change = (
        jnp.einsum("bkgj,bkgd->bjkd", score_grad, q_heads, preferred_element_type=jnp.float32)
        .astype(jnp.bfloat16)
        .reshape(sub_count * seq_len, kv_local * HEAD_DIM)
    )
    value_adapter_change = (
        jnp.einsum("bkgj,bkgd->bjkd", prob_half, grad_heads, preferred_element_type=jnp.float32)
        .astype(jnp.bfloat16)
        .reshape(sub_count * seq_len, kv_local * HEAD_DIM)
    )
    last_part = final_product(query_delta, wq_full)
    key_coefficient = final_product(key_adapter_change, key_up_matrix).astype(jnp.bfloat16)
    value_coefficient = final_product(value_adapter_change, value_up_matrix).astype(jnp.bfloat16)
    input_portion = final_product(key_adapter_change, key_weight_matrix) + final_product(
        value_adapter_change, value_weight_matrix
    )
    input_portion = input_portion + ADAPTER_SCALE * (
        final_product(key_coefficient, key_down_matrix)
        + final_product(value_coefficient, value_down)
    )
    input_portion = input_portion.at[last_rows].add(last_part)
    input_sum = lax.psum_scatter(
        input_portion.astype(jnp.bfloat16), "mp", scatter_dimension=1, tiled=True
    ).astype(jnp.float32)
    input_sum = input_sum.at[last_rows].add(cot_local.astype(jnp.float32))
    input_grad = input_sum.astype(jnp.bfloat16).reshape(hidden_in.shape)
    key_down_grad, value_down_grad = lax.psum(
        (
            ADAPTER_SCALE * first_product(token_inputs, key_coefficient),
            ADAPTER_SCALE * first_product(token_inputs, value_coefficient),
        ),
        ("dp", "mp"),
    )
    total_loss, key_up_grad, value_up_grad = lax.psum(
        (
            loss_part,
            ADAPTER_SCALE * first_product(reduced_key, key_adapter_change),
            ADAPTER_SCALE * first_product(reduced_value, value_adapter_change),
        ),
        "dp",
    )
    mean_loss = total_loss / batch_size
    return (
        mean_loss,
        query_grad,
        item_grad,
        input_grad,
        key_down_grad,
        value_down_grad,
        key_up_grad,
        value_up_grad,
    )


TILE = 512
EMB, XS, SC, RES, QP, AP, GB, QD, LP, DN, DNG = range(11)
M_X, M_COEF, M_PART, M_LAST, M_DN = range(5)


def plain_product(left_side, right_side):
    return jnp.dot(left_side, right_side, preferred_element_type=jnp.float32)


def step_kernel(
    dp, mp, subs, rank, names, *refs,
):
    r = dict(zip(names, refs, strict=True))
    len_ref, pair_ref, hard_ref = r["lengths"], r["pair"], r["hard"]
    q_ref, item_ref, x_hbm, kup_ref, vup_ref = r["q"], r["item"], r["x"], r["kup"], r["vup"]
    xg, wq, wk, wv, wo, down = r["xg"], r["wq"], r["wk"], r["wv"], r["wo"], r["down"]
    ssem, rsem, msend, mrecv, csem = r["ssem"], r["rsem"], r["msend"], r["mrecv"], r["csem"]
    me = lax.axis_index("dp")
    core = lax.axis_index("mp")
    other = 1 - core
    rows, feats = x_hbm.shape
    seq_len = rows // subs
    local_rows = q_ref.shape[0]
    batch = dp * local_rows
    dq, qw = wq.shape
    tiles = feats // TILE
    per_core = dp // mp
    home = me // per_core
    slot = lax.rem(me, per_core)
    at_home = core == home
    mesh_id = pl.DeviceIdType.MESH
    f32, bf16 = jnp.float32, jnp.bfloat16

    local_copies = [
        pltpu.make_async_copy(src, dst, csem.at[i])
        for i, (src, dst) in enumerate(
            (
                (x_hbm, xg.at[core]),
                (r["wq_hbm"], wq),
                (r["wk_hbm"], wk),
                (r["wv_hbm"], wv),
                (r["wo_hbm"], wo),
                (r["kdown"], down.at[pl.ds(0, rank)]),
                (r["vdown"], down.at[pl.ds(rank, rank)]),
            )
        )
    ]
    for copy in local_copies:
        copy.start()

    barrier = pltpu.get_barrier_semaphore()

    @pl.loop(1, dp * mp)
    def _(n):
        flat = lax.rem(me * mp + core + n, dp * mp)
        pl.semaphore_signal(
            barrier, inc=1, device_id=(flat // mp, lax.rem(flat, mp)), device_id_type=mesh_id
        )

    es, emb_land = r["es"], r["emb_land"]
    both = jnp.concatenate([q_ref[...].astype(f32), item_ref[...].astype(f32)], axis=0)
    for c in range(per_core):
        es[c] = both[:, c * dq : (c + 1) * dq].astype(bf16)
    pl.semaphore_wait(barrier, dp * mp - 1)

    def remote(source, landing, send, recv, target, target_core):
        return pltpu.make_async_remote_copy(
            src_ref=source,
            dst_ref=landing,
            send_sem=send,
            recv_sem=recv,
            device_id=(target, target_core),
            device_id_type=mesh_id,
        )

    def slice_copy(op, n, source, landing):
        return remote(
            source.at[n // mp], landing.at[me], ssem.at[op, n], rsem.at[op, me],
            core * per_core + n // mp, lax.rem(n, mp),
        )

    def is_self(n):
        return (core * per_core + n // mp == me) & (lax.rem(n, mp) == core)

    def slice_start(op, source, landing):
        @pl.loop(0, dp)
        def _(n):
            @pl.when(jnp.logical_not(is_self(n)))
            def _():
                slice_copy(op, n, source, landing).start()

        @pl.when(at_home)
        def _():
            landing[me] = source[slot]

    def slice_wait(op, source, landing):
        @pl.loop(0, dp)
        def _(n):
            @pl.when(jnp.logical_not(is_self(n)))
            def _():
                slice_copy(op, n, source, landing).wait_send()

            @pl.when(jnp.logical_not(at_home & (n == me)))
            def _():
                remote(
                    source.at[0], landing.at[n], ssem.at[op, 0], rsem.at[op, n], me, other
                ).wait_recv()

    def dp_copy(op, k, source, landing):
        target = lax.rem(me + k, dp)
        return remote(
            source(target), landing.at[me], ssem.at[op, k], rsem.at[op, k], target, core
        )

    def dp_start(op, source, landing):
        @pl.loop(1, dp)
        def _(k):
            dp_copy(op, k, source, landing).start()

    def dp_wait(op, source, landing):
        @pl.loop(1, dp)
        def _(k):
            dp_copy(op, k, source, landing).wait()

    def mp_copy(op, source, landing):
        return remote(source, landing, msend.at[op], mrecv.at[op], me, other)

    def total_of(landing):
        total = landing[0]
        for j in range(1, dp):
            total = total + landing[j]
        return total

    emb_args = (EMB, es, emb_land)
    slice_start(*emb_args)

    local_copies[0].wait()
    last = [jnp.clip(len_ref[b] - 1, 0, seq_len - 1) + b * seq_len for b in range(subs)]
    one_row = lax.broadcasted_iota(jnp.int32, (8, rows), 0)
    one_col = lax.broadcasted_iota(jnp.int32, (8, rows), 1)
    picked_rows = jnp.zeros((8, rows), f32)
    for b in range(subs):
        picked_rows = jnp.where((one_row == b) & (one_col == last[b]), 1.0, picked_rows)
    last_tokens = plain_product(picked_rows.astype(bf16), xg[core])[:subs]
    xs, x_land = r["xs"], r["x_land"]
    for c in range(per_core):
        xs[c] = last_tokens[:, c * dq : (c + 1) * dq]
    xs_args = (XS, xs, x_land)
    slice_start(*xs_args)
    x_copy = mp_copy(M_X, xg.at[core], xg.at[core])
    x_copy.start()

    slice_wait(*emb_args)
    emb = emb_land[...].astype(f32)
    queries = emb[:, :local_rows].reshape(batch, dq).astype(bf16)
    items = emb[:, local_rows:].reshape(batch, dq).astype(bf16)
    sc, sc_land = r["sc"], r["sc_land"]
    sc[...] = final_product(queries, items).reshape(dp, local_rows, batch)
    sc_args = (SC, lambda t: sc.at[t], sc_land)
    dp_start(*sc_args)
    sc_land[me] = sc[me]

    slice_wait(*xs_args)
    x_rows = r["x_rows"]
    for j in range(dp):
        x_rows[j * subs : (j + 1) * subs, :] = x_land[j]
    local_copies[1].wait()
    part_q, land_q = r["part_q"], r["land_q"]
    query_part = plain_product(x_rows[...].astype(bf16), wq[...])
    for j in range(dp):
        part_q[j] = query_part[j * subs : (j + 1) * subs]

    columns = lax.broadcasted_iota(jnp.int32, (local_rows, batch), 1)
    row_ids = lax.broadcasted_iota(jnp.int32, (local_rows, batch), 0)
    hard_count = jnp.zeros((local_rows, batch), f32)
    target = jnp.zeros((local_rows, batch), f32)
    for i in range(local_rows):
        for h in range(hard_ref.shape[0]):
            hit = (row_ids == i) & (columns == hard_ref[h, i])
            hard_count = hard_count + jnp.where(hit, 1.0, 0.0)
        target = jnp.where((row_ids == i) & (columns == pair_ref[i]), 1.0, target)
    dp_wait(*sc_args)
    logits = total_of(sc_land) * INV_TEMP + HARD_NEGATIVE_ADD * hard_count
    row_top = jnp.max(logits, axis=1, keepdims=True)
    log_total = row_top + jnp.log(jnp.sum(jnp.exp(logits - row_top), axis=1, keepdims=True))
    picked = jnp.sum(target * logits, axis=1, keepdims=True)
    loss_part = jnp.sum(log_total - picked, axis=0, keepdims=True)
    residual = (jnp.exp(logits - log_total) - target).astype(bf16).astype(f32)
    res_own, res_land = r["res_own"], r["res_land"]
    res_own[...] = residual
    res_args = (RES, lambda t: res_own, res_land)
    dp_start(*res_args)
    res_land[me] = residual
    q_args = (QP, lambda t: part_q.at[t], land_q)
    dp_start(*q_args)
    land_q[me] = part_q[me]

    acc_k, acc_v, acc_low = r["acc_k"], r["acc_v"], r["acc_low"]
    acc_k[...] = jnp.zeros_like(acc_k)
    acc_v[...] = jnp.zeros_like(acc_v)
    acc_low[...] = jnp.zeros_like(acc_low)
    for i in (2, 3, 5, 6):
        local_copies[i].wait()

    def project(which):
        @pl.loop(0, tiles)
        def _(t):
            cols = pl.ds(pl.multiple_of(t * TILE, TILE), TILE)
            spot = pl.ds(pl.multiple_of(which * feats + t * TILE, TILE), TILE)
            block = xg[which, :, cols]
            acc_k[...] += plain_product(block, wk[spot, :])
            acc_v[...] += plain_product(block, wv[spot, :])
            acc_low[...] += final_product(block, down[:, spot])

    project(core)

    dp_wait(*res_args)
    res = res_land[...].reshape(batch, batch)
    query_grad = plain_product(res.astype(bf16), items) * INV_TEMP
    item_grad = (plain_product(res.T.astype(bf16), queries) * INV_TEMP).astype(bf16).astype(f32)
    item_slabs = item_grad.reshape(dp, local_rows, dq)
    cot_rows = r["cot_rows"]
    for j in range(dp):
        cot_rows[j * subs : (j + 1) * subs, :] = item_slabs[j, :subs]
    local_copies[4].wait()
    part_a, land_a = r["part_a"], r["land_a"]
    grad_part = final_product(cot_rows[...].astype(bf16), wo[...])
    for j in range(dp):
        part_a[j] = grad_part[j * subs : (j + 1) * subs]
    a_args = (AP, lambda t: part_a.at[t], land_a)
    dp_start(*a_args)
    land_a[me] = part_a[me]
    gs, g_land = r["gs"], r["g_land"]
    gs[...] = jnp.concatenate(
        [query_grad.reshape(dp, local_rows, dq), item_slabs], axis=1
    ).astype(bf16)

    def back_copy(k):
        to = lax.rem(me + k, dp)
        return remote(gs.at[to], g_land.at[slot], ssem.at[GB, k], rsem.at[GB, slot], to, core)

    @pl.when(at_home)
    def _():
        @pl.loop(1, dp)
        def _(k):
            back_copy(k).start()

        g_land[slot] = gs[me]

    x_copy.wait()
    project(other)
    low = acc_low[...].astype(bf16)
    low_key, low_value = low[:, :rank], low[:, rank:]
    keys = (acc_k[...] + ADAPTER_SCALE * plain_product(low_key, kup_ref[...])).astype(bf16)
    values = (acc_v[...] + ADAPTER_SCALE * plain_product(low_value, vup_ref[...])).astype(bf16)

    heads = qw // HEAD_DIM
    group_size = HEADS // KV_HEADS
    score_scale = 1.0 / math.sqrt(HEAD_DIM)

    def spread(flat, blocks):
        blocks[...] = jnp.zeros_like(blocks)
        for b in range(subs):
            for h in range(heads):
                kv = h // group_size * HEAD_DIM
                blocks[b * heads + h : b * heads + h + 1, kv : kv + HEAD_DIM] = flat[
                    b : b + 1, h * HEAD_DIM : (h + 1) * HEAD_DIM
                ]
        return blocks[...].astype(bf16)

    dp_wait(*q_args)
    r["flat_q"][...] = total_of(land_q).astype(bf16).astype(f32)
    q_half = spread(r["flat_q"], r["q_blk"])
    raw = final_product(q_half, keys) * score_scale
    head_rows = lax.broadcasted_iota(jnp.int32, raw.shape, 0)
    token_ids = lax.broadcasted_iota(jnp.int32, raw.shape, 1)
    live = jnp.zeros(raw.shape, jnp.bool_)
    for b in range(subs):
        mine = (head_rows >= b * heads) & (head_rows < (b + 1) * heads)
        live = live | (mine & (token_ids >= b * seq_len) & (token_ids <= last[b]))
    raw = jnp.where(live, raw, -jnp.inf)
    weights = jnp.exp(raw - jnp.max(raw, axis=1, keepdims=True))
    probs = weights / jnp.sum(weights, axis=1, keepdims=True)
    dp_wait(*a_args)
    r["flat_a"][...] = total_of(land_a).astype(bf16).astype(f32)
    g_half = spread(r["flat_a"], r["g_blk"])
    prob_grad = final_product(g_half, values)
    score_grad = (
        probs * (prob_grad - jnp.sum(probs * prob_grad, axis=1, keepdims=True)) * score_scale
    ).astype(bf16)

    query_delta = plain_product(score_grad, keys)
    qd_f, qd_own, qd_all = r["qd_f"], r["qd_own"], r["qd_all"]
    blocks = qw // dq
    in_block = dq // HEAD_DIM
    for b in range(subs):
        for h in range(heads):
            kv = h // group_size * HEAD_DIM
            spot = b * blocks + h // in_block
            lane = h % in_block * HEAD_DIM
            qd_f[spot : spot + 1, lane : lane + HEAD_DIM] = query_delta[
                b * heads + h : b * heads + h + 1, kv : kv + HEAD_DIM
            ]
    qd_own[...] = qd_f[...].astype(bf16)
    qd_args = (QD, lambda t: qd_own, qd_all)
    dp_start(*qd_args)
    qd_all[me] = qd_own[...]

    key_delta = first_product(score_grad, q_half).astype(bf16)
    value_delta = first_product(probs.astype(bf16), g_half).astype(bf16)
    coef = jnp.concatenate(
        [final_product(key_delta, kup_ref[...]), final_product(value_delta, vup_ref[...])], axis=1
    ).astype(bf16)
    coef_g = r["coef_g"]
    coef_g[core] = coef
    coef_copy = mp_copy(M_COEF, coef_g.at[core], coef_g.at[core])
    coef_copy.start()

    dn, dn_land, dn_all = r["dn"], r["dn_land"], r["dn_all"]
    up_grad = ADAPTER_SCALE * jnp.concatenate(
        [first_product(low_key, key_delta), first_product(low_value, value_delta)], axis=0
    )
    lane_groups = up_grad.shape[1] // 128
    cols = feats // dp
    own_down = first_product(coef, xg[core])
    for j in range(dp):
        top = j // lane_groups * 8
        lane = j % lane_groups * 128
        dn[j, 2 * rank :, :] = up_grad[top : top + 8, lane : lane + 128]
    coef_copy.wait()
    down_part = ADAPTER_SCALE * (own_down + first_product(coef_g[other], xg[core]))
    for j in range(dp):
        dn[j, : 2 * rank, :] = down_part[:, j * cols : (j + 1) * cols]
    dn_args = (DN, lambda t: dn.at[t], dn_land)
    dp_start(*dn_args)
    dn_land[me] = dn[me]

    pacc, pbuf, p_land, last_f = r["pacc"], r["pbuf"], r["p_land"], r["last_f"]

    def portion(which, place):
        @pl.loop(0, tiles)
        def _(t):
            cols = pl.ds(pl.multiple_of(t * TILE, TILE), TILE)
            spot = pl.ds(pl.multiple_of(which * feats + t * TILE, TILE), TILE)
            pacc[...] = (
                final_product(key_delta, wk[spot, :])
                + final_product(value_delta, wv[spot, :])
                + ADAPTER_SCALE * plain_product(coef, down[:, spot])
            )
            pbuf[place, :, cols] = pacc[...].astype(bf16)
            for b in range(subs):
                last_f[place, b : b + 1, cols] = pacc[pl.ds(last[b], 1), :]

    portion(other, 1)
    part_copy = mp_copy(M_PART, pbuf.at[1], p_land)
    part_copy.start()

    dp_wait(*qd_args)
    changes = qd_all[...].reshape(dp * subs * blocks, dq)
    block_ids = lax.rem(lax.broadcasted_iota(jnp.int32, (dp * subs * blocks, dq), 0), blocks)
    last_part = jnp.zeros((dp * subs * blocks, dq), f32)
    for c in range(blocks):
        term = final_product(changes, wq[:, c * dq : (c + 1) * dq])
        last_part = jnp.where(block_ids == c, term, last_part)
    last_part = jnp.sum(last_part.reshape(dp * subs, blocks, dq), axis=1)
    lp, lp_land = r["lp"], r["lp_land"]
    for j in range(dp):
        lp[j, :subs] = last_part[j * subs : (j + 1) * subs]
        lp[j, subs:] = jnp.broadcast_to(loss_part, (lp.shape[1] - subs, dq))
    lp_args = (LP, lambda t: lp.at[t], lp_land)
    dp_start(*lp_args)
    lp_land[me] = lp[me]

    dp_wait(*dn_args)
    dn_all[core, me] = total_of(dn_land)
    dng_args = (DNG, lambda t: dn_all.at[core, me], dn_all.at[core])
    dp_start(*dng_args)

    portion(core, 0)

    @pl.when(at_home)
    def _():
        @pl.loop(1, dp)
        def _(k):
            back_copy(k).wait_send()

    @pl.loop(0, per_core)
    def _(c):
        @pl.when(core * per_core + c != me)
        def _():
            remote(
                gs.at[0], g_land.at[c], ssem.at[GB, 0], rsem.at[GB, c], me, other
            ).wait_recv()

    cot = r["cot"]
    for c in range(per_core):
        span = slice(c * dq, (c + 1) * dq)
        slab = g_land[c].astype(f32)
        r["q_grad"][:, span] = slab[:local_rows].astype(bf16)
        r["item_grad"][:, span] = slab[local_rows:].astype(bf16)
        cot[:, span] = slab[local_rows : local_rows + subs]

    dp_wait(*lp_args)
    last_total, last_send, last_land = r["last_total"], r["last_send"], r["last_land"]
    loss = lp_land[0, subs : subs + 1, 0:1]
    for j in range(1, dp):
        loss = loss + lp_land[j, subs : subs + 1, 0:1]
    r["loss"][...] = loss / batch
    for which in range(mp):
        for c in range(per_core):
            last_total[which, :, c * dq : (c + 1) * dq] = lp_land[which * per_core + c, :subs]
    last_send[...] = (last_f[1] + last_total[other]).astype(bf16).astype(f32)
    last_copy = mp_copy(M_LAST, last_send, last_land)
    last_copy.start()
    dp_wait(*dng_args)
    down_copy = mp_copy(M_DN, dn_all.at[core], dn_all.at[core])
    down_copy.start()

    own_last = (last_f[0] + last_total[core]).astype(bf16).astype(f32)
    last_copy.wait()
    last_f[0] = own_last + last_land[...] + cot[...]
    part_copy.wait()

    @pl.loop(0, tiles)
    def _(t):
        cols = pl.ds(pl.multiple_of(t * TILE, TILE), TILE)
        both = pbuf[0, :, cols].astype(f32) + p_land[:, cols].astype(f32)
        ids = lax.broadcasted_iota(jnp.int32, both.shape, 0)
        for b in range(subs):
            both = jnp.where(ids == last[b], last_f[0, b : b + 1, cols], both)
        r["input_grad"][:, cols] = both.astype(bf16)

    for j in range(dp):
        top = j // lane_groups * 8
        lane = j % lane_groups * 128
        out = r["key_up"] if top < rank else r["value_up"]
        out[top % rank : top % rank + 8, lane : lane + 128] = dn_all[core, j, 2 * rank :, :]
    down_copy.wait()
    for which in range(mp):
        for j in range(dp):
            span = slice(which * feats + j * cols, which * feats + (j + 1) * cols)
            r["key_down"][:, span] = dn_all[which, j, :rank, :]
            r["value_down"][:, span] = dn_all[which, j, rank : 2 * rank, :]


def fused_local(
    query_emb, item_emb, pair_index, hard_index, hidden_in, lengths, w_query, key_weight_matrix,
    value_weight_matrix, w_out, key_down_matrix, key_up_matrix, value_down, value_up_matrix,
):
    dp, mp = lax.axis_size("dp"), lax.axis_size("mp")
    local_rows, feats = query_emb.shape
    subs, _, seq_len, _ = hidden_in.shape
    rows = subs * seq_len
    rank, kw = key_up_matrix.shape
    dq, qw = w_query.shape
    width = feats * mp
    heads = qw // HEAD_DIM
    batch = dp * local_rows
    per_core = dp // mp
    blocks = qw // dq
    slab = 2 * rank + 8
    f32, bf16 = jnp.float32, jnp.bfloat16
    vmem, hbm = pl.BlockSpec(memory_space=pltpu.VMEM), pl.BlockSpec(memory_space=pl.ANY)
    smem = pl.BlockSpec(memory_space=pltpu.SMEM)
    inputs = {
        "lengths": (lengths[:, 0], smem),
        "pair": (pair_index, smem),
        "hard": (hard_index.T, smem),
        "q": (query_emb, vmem),
        "item": (item_emb, vmem),
        "x": (hidden_in.reshape(rows, feats), hbm),
        "wq_hbm": (w_query, hbm),
        "wk_hbm": (key_weight_matrix, hbm),
        "wv_hbm": (value_weight_matrix, hbm),
        "wo_hbm": (w_out, hbm),
        "kdown": (key_down_matrix.T, hbm),
        "vdown": (value_down.T, hbm),
        "kup": (key_up_matrix, vmem),
        "vup": (value_up_matrix, vmem),
    }
    outputs = {
        "loss": ((1, 1), f32),
        "q_grad": ((local_rows, feats), bf16),
        "item_grad": ((local_rows, feats), bf16),
        "input_grad": ((rows, feats), bf16),
        "key_down": ((rank, width), f32),
        "value_down": ((rank, width), f32),
        "key_up": ((rank, kw), f32),
        "value_up": ((rank, kw), f32),
    }
    scratch = {
        "es": ((per_core, 2 * local_rows, dq), bf16),
        "emb_land": ((dp, 2 * local_rows, dq), bf16),
        "xs": ((per_core, subs, dq), f32),
        "x_land": ((dp, subs, dq), f32),
        "x_rows": ((dp * subs, dq), f32),
        "sc": ((dp, local_rows, batch), f32),
        "sc_land": ((dp, local_rows, batch), f32),
        "res_own": ((local_rows, batch), f32),
        "res_land": ((dp, local_rows, batch), f32),
        "part_q": ((dp, subs, qw), f32),
        "land_q": ((dp, subs, qw), f32),
        "cot_rows": ((dp * subs, dq), f32),
        "part_a": ((dp, subs, qw), f32),
        "land_a": ((dp, subs, qw), f32),
        "gs": ((dp, 2 * local_rows, dq), bf16),
        "g_land": ((per_core, 2 * local_rows, dq), bf16),
        "cot": ((subs, feats), f32),
        "xg": ((mp, rows, feats), bf16),
        "wq": ((dq, qw), bf16),
        "wk": ((width, kw), bf16),
        "wv": ((width, kw), bf16),
        "wo": ((qw, dq), bf16),
        "down": ((2 * rank, width), bf16),
        "acc_k": ((rows, kw), f32),
        "acc_v": ((rows, kw), f32),
        "acc_low": ((rows, 2 * rank), f32),
        "q_blk": ((subs * heads, kw), f32),
        "g_blk": ((subs * heads, kw), f32),
        "flat_q": ((subs, qw), f32),
        "flat_a": ((subs, qw), f32),
        "qd_f": ((subs * blocks, dq), f32),
        "qd_own": ((subs * blocks, dq), bf16),
        "qd_all": ((dp, subs * blocks, dq), bf16),
        "lp": ((dp, 2 * subs, dq), f32),
        "lp_land": ((dp, 2 * subs, dq), f32),
        "coef_g": ((mp, rows, 2 * rank), bf16),
        "pacc": ((rows, TILE), f32),
        "pbuf": ((2, rows, feats), bf16),
        "p_land": ((rows, feats), bf16),
        "last_f": ((2, subs, feats), f32),
        "last_total": ((mp, subs, feats), f32),
        "last_send": ((subs, feats), f32),
        "last_land": ((subs, feats), f32),
        "dn": ((dp, slab, feats // dp), f32),
        "dn_land": ((dp, slab, feats // dp), f32),
        "dn_all": ((mp, dp, slab, feats // dp), f32),
    }
    sems = {"ssem": (11, dp), "rsem": (11, dp), "msend": (5,), "mrecv": (5,), "csem": (7,)}
    names = (*inputs, *outputs, *scratch, *sems)
    out = pl.pallas_call(
        functools.partial(step_kernel, dp, mp, subs, rank, names),
        out_shape=tuple(jax.ShapeDtypeStruct(s, t) for s, t in outputs.values()),
        in_specs=[spec for _, spec in inputs.values()],
        out_specs=(vmem,) * len(outputs),
        scratch_shapes=[pltpu.VMEM(s, t) for s, t in scratch.values()]
        + [pltpu.SemaphoreType.DMA(s) for s in sems.values()],
        compiler_params=pltpu.CompilerParams(
            collective_id=0, has_side_effects=True, vmem_limit_bytes=60 * 1024 * 1024
        ),
    )(*(value for value, _ in inputs.values()))
    loss, query_grad, item_grad, input_grad, key_down, value_down_grad, key_up, value_up = out
    return (
        loss[0, 0],
        query_grad,
        item_grad,
        input_grad.reshape(hidden_in.shape),
        key_down.T,
        value_down_grad.T,
        key_up,
        value_up,
    )


def solution(mesh):
    in_specs = (
        P("dp", "mp"),
        P("dp", "mp"),
        P("dp"),
        P("dp", None),
        P(None, "dp", None, "mp"),
        P(None, "dp"),
        P("dp", "mp"),
        P(None, "mp"),
        P(None, "mp"),
        P("mp", "dp"),
        P(),
        P(None, "mp"),
        P(),
        P(None, "mp"),
    )
    out_specs = (
        P(),
        P("dp", "mp"),
        P("dp", "mp"),
        P(None, "dp", None, "mp"),
        P(),
        P(),
        P(None, "mp"),
        P(None, "mp"),
    )
    small = mesh.shape["mp"] == 2 and mesh.shape["dp"] == 16
    body = fused_local if small else local
    return jax.shard_map(body, mesh=mesh, in_specs=in_specs, out_specs=out_specs, check_vma=False)
```

```python
import functools
import math

import jax
import jax.numpy as jnp
from jax import lax
from jax.experimental import pallas as pl
from jax.experimental.pallas import tpu as pltpu
from jax.sharding import PartitionSpec as P

HEADS = 32
KV_HEADS = 8
HEAD_DIM = 128


INV_TEMP = 50.0
HARD_NEGATIVE_ADD = 4.0
ADAPTER_SCALE = 2.0


def final_product(left_side, right_side):
    return lax.dot_general(
        left_side, right_side, (((1,), (1,)), ((), ())), preferred_element_type=jnp.float32
    )


def first_product(left_side, right_side):
    return lax.dot_general(
        left_side, right_side, (((0,), (0,)), ((), ())), preferred_element_type=jnp.float32
    )


def local(
    query_emb,
    item_emb,
    pair_index,
    hard_index,
    hidden_in,
    lengths,
    w_query,
    key_weight_matrix,
    value_weight_matrix,
    w_out,
    key_down_matrix,
    key_up_matrix,
    value_down,
    value_up_matrix,
):
    dp_count = lax.axis_size("dp")
    local_rows = query_emb.shape[0]
    batch_size = local_rows * dp_count
    items_all = lax.all_gather(item_emb, "dp", axis=0, tiled=True)
    partial_scores = final_product(query_emb, items_all)
    pair_scores = lax.psum(partial_scores, "mp") * INV_TEMP
    columns = jnp.arange(batch_size, dtype=jnp.int32)
    hard_negative_count = jnp.sum(
        (hard_index[:, :, None] == columns[None, None, :]).astype(jnp.float32), axis=1
    )
    score_logits = pair_scores + HARD_NEGATIVE_ADD * hard_negative_count
    row_top = jnp.max(score_logits, axis=1, keepdims=True)
    log_total = row_top[:, 0] + jnp.log(jnp.sum(jnp.exp(score_logits - row_top), axis=1))
    target = (pair_index[:, None] == columns[None, :]).astype(jnp.float32)
    picked = jnp.sum(target * score_logits, axis=1)
    loss_part = jnp.sum(log_total - picked)
    residual = (jnp.exp(score_logits - log_total[:, None]) - target).astype(jnp.bfloat16)
    query_grad = (
        jnp.dot(residual, items_all, preferred_element_type=jnp.float32) * INV_TEMP
    ).astype(jnp.bfloat16)
    item_grad = lax.psum_scatter(
        first_product(residual, query_emb) * INV_TEMP, "dp", scatter_dimension=0, tiled=True
    ).astype(jnp.bfloat16)
    sub_count = hidden_in.shape[0]
    seq_len = hidden_in.shape[2]
    full_rows = lax.all_gather(hidden_in, "mp", axis=3, tiled=True)
    model_width = full_rows.shape[3]
    token_inputs = full_rows.reshape(sub_count * seq_len, model_width)
    seq_lengths = lengths[:, 0]
    last_rows = jnp.arange(sub_count, dtype=jnp.int32) * seq_len + seq_lengths - 1
    last_tokens = jnp.take(token_inputs, last_rows, axis=0)
    cot_local = item_grad[:sub_count]
    cot_full = lax.all_gather(cot_local, "mp", axis=1, tiled=True)
    adapter_rank = key_down_matrix.shape[1]
    down_both = jnp.concatenate([key_down_matrix, value_down], axis=1)
    reduced_pair = jnp.dot(token_inputs, down_both, preferred_element_type=jnp.float32).astype(
        jnp.bfloat16
    )
    reduced_key = reduced_pair[:, :adapter_rank]
    reduced_value = reduced_pair[:, adapter_rank:]
    key_rows = (
        jnp.dot(token_inputs, key_weight_matrix, preferred_element_type=jnp.float32)
        + ADAPTER_SCALE * jnp.dot(reduced_key, key_up_matrix, preferred_element_type=jnp.float32)
    ).astype(jnp.bfloat16)
    value_rows = (
        jnp.dot(token_inputs, value_weight_matrix, preferred_element_type=jnp.float32)
        + ADAPTER_SCALE
        * jnp.dot(reduced_value, value_up_matrix, preferred_element_type=jnp.float32)
    ).astype(jnp.bfloat16)
    query_width = w_query.shape[1]
    wq_full, wo_full = (
        lax.all_gather(w_query, "dp", axis=0, tiled=True),
        lax.all_gather(w_out, "dp", axis=1, tiled=True),
    )
    query = jnp.dot(last_tokens, wq_full, preferred_element_type=jnp.float32).astype(jnp.bfloat16)
    attn_grad = final_product(cot_full, wo_full).astype(jnp.bfloat16)
    group_size = HEADS // KV_HEADS
    kv_local = key_rows.shape[1] // HEAD_DIM
    score_scale = 1.0 / math.sqrt(HEAD_DIM)
    q_heads = query.reshape(sub_count, kv_local, group_size, HEAD_DIM)
    k_heads = key_rows.reshape(sub_count, seq_len, kv_local, HEAD_DIM)
    v_heads = value_rows.reshape(sub_count, seq_len, kv_local, HEAD_DIM)
    raw_scores = (
        jnp.einsum("bkgd,bjkd->bkgj", q_heads, k_heads, preferred_element_type=jnp.float32)
        * score_scale
    )
    live_mask = jnp.arange(seq_len, dtype=jnp.int32)[None, :] < seq_lengths[:, None]
    raw_scores = jnp.where(live_mask[:, None, None, :], raw_scores, -jnp.inf)
    row_peak = jnp.max(raw_scores, axis=-1, keepdims=True)
    weights = jnp.exp(raw_scores - row_peak)
    softmax_probs = weights / jnp.sum(weights, axis=-1, keepdims=True)
    prob_half = softmax_probs.astype(jnp.bfloat16)
    grad_heads = attn_grad.reshape(sub_count, kv_local, group_size, HEAD_DIM)
    prob_grad = jnp.einsum(
        "bkgd,bjkd->bkgj", grad_heads, v_heads, preferred_element_type=jnp.float32
    )
    score_grad = (
        softmax_probs
        * (prob_grad - jnp.sum(softmax_probs * prob_grad, axis=-1, keepdims=True))
        * score_scale
    ).astype(jnp.bfloat16)
    query_delta = (
        jnp.einsum("bkgj,bjkd->bkgd", score_grad, k_heads, preferred_element_type=jnp.float32)
        .astype(jnp.bfloat16)
        .reshape(sub_count, query_width)
    )
    key_adapter_change = (
        jnp.einsum("bkgj,bkgd->bjkd", score_grad, q_heads, preferred_element_type=jnp.float32)
        .astype(jnp.bfloat16)
        .reshape(sub_count * seq_len, kv_local * HEAD_DIM)
    )
    value_adapter_change = (
        jnp.einsum("bkgj,bkgd->bjkd", prob_half, grad_heads, preferred_element_type=jnp.float32)
        .astype(jnp.bfloat16)
        .reshape(sub_count * seq_len, kv_local * HEAD_DIM)
    )
    last_part = final_product(query_delta, wq_full)
    key_coefficient = final_product(key_adapter_change, key_up_matrix).astype(jnp.bfloat16)
    value_coefficient = final_product(value_adapter_change, value_up_matrix).astype(jnp.bfloat16)
    input_portion = final_product(key_adapter_change, key_weight_matrix) + final_product(
        value_adapter_change, value_weight_matrix
    )
    input_portion = input_portion + ADAPTER_SCALE * (
        final_product(key_coefficient, key_down_matrix)
        + final_product(value_coefficient, value_down)
    )
    input_portion = input_portion.at[last_rows].add(last_part)
    input_sum = lax.psum_scatter(
        input_portion.astype(jnp.bfloat16), "mp", scatter_dimension=1, tiled=True
    ).astype(jnp.float32)
    input_sum = input_sum.at[last_rows].add(cot_local.astype(jnp.float32))
    input_grad = input_sum.astype(jnp.bfloat16).reshape(hidden_in.shape)
    key_down_grad, value_down_grad = lax.psum(
        (
            ADAPTER_SCALE * first_product(token_inputs, key_coefficient),
            ADAPTER_SCALE * first_product(token_inputs, value_coefficient),
        ),
        ("dp", "mp"),
    )
    total_loss, key_up_grad, value_up_grad = lax.psum(
        (
            loss_part,
            ADAPTER_SCALE * first_product(reduced_key, key_adapter_change),
            ADAPTER_SCALE * first_product(reduced_value, value_adapter_change),
        ),
        "dp",
    )
    mean_loss = total_loss / batch_size
    return (
        mean_loss,
        query_grad,
        item_grad,
        input_grad,
        key_down_grad,
        value_down_grad,
        key_up_grad,
        value_up_grad,
    )


TILE = 1024
EMB, XS, SC, RES, QP, AP, GB, QD, LP, DN, DNG = range(11)
M_X, M_COEF, M_PART, M_LAST, M_DN = range(5)


def plain_product(left_side, right_side):
    return jnp.dot(left_side, right_side, preferred_element_type=jnp.float32)


def step_kernel(
    dp, mp, subs, rank, names, *refs,
):
    r = dict(zip(names, refs, strict=True))
    len_ref, pair_ref, hard_ref = r["lengths"], r["pair"], r["hard"]
    q_ref, item_ref, x_hbm, kup_ref, vup_ref = r["q"], r["item"], r["x"], r["kup"], r["vup"]
    xg, wq, wkv, wo, down = r["xg"], r["wq"], r["wkv"], r["wo"], r["down"]
    ssem, rsem, msend, mrecv, csem = r["ssem"], r["rsem"], r["msend"], r["mrecv"], r["csem"]
    me = lax.axis_index("dp")
    core = lax.axis_index("mp")
    other = 1 - core
    rows, feats = x_hbm.shape
    seq_len = rows // subs
    local_rows = q_ref.shape[0]
    batch = dp * local_rows
    dq, qw = wq.shape
    kw = wkv.shape[1] // 2
    tiles = feats // TILE
    per_core = dp // mp
    home = me // per_core
    slot = lax.rem(me, per_core)
    at_home = core == home
    mesh_id = pl.DeviceIdType.MESH
    f32, bf16 = jnp.float32, jnp.bfloat16

    local_copies = [
        pltpu.make_async_copy(src, dst, csem.at[i])
        for i, (src, dst) in enumerate(
            (
                (x_hbm, xg.at[core]),
                (r["wq_hbm"], wq),
                (r["wk_hbm"], wkv.at[:, pl.ds(0, kw)]),
                (r["wv_hbm"], wkv.at[:, pl.ds(kw, kw)]),
                (r["wo_hbm"], wo),
                (r["kdown"], down.at[pl.ds(0, rank)]),
                (r["vdown"], down.at[pl.ds(rank, rank)]),
            )
        )
    ]
    for copy in local_copies:
        copy.start()

    barrier = pltpu.get_barrier_semaphore()

    @pl.loop(1, dp * mp)
    def _(n):
        flat = lax.rem(me * mp + core + n, dp * mp)
        pl.semaphore_signal(
            barrier, inc=1, device_id=(flat // mp, lax.rem(flat, mp)), device_id_type=mesh_id
        )

    es, emb_land = r["es"], r["emb_land"]
    both = jnp.concatenate([q_ref[...].astype(f32), item_ref[...].astype(f32)], axis=0)
    for c in range(per_core):
        es[c] = both[:, c * dq : (c + 1) * dq].astype(bf16)
    pl.semaphore_wait(barrier, dp * mp - 1)

    def remote(source, landing, send, recv, target, target_core):
        return pltpu.make_async_remote_copy(
            src_ref=source,
            dst_ref=landing,
            send_sem=send,
            recv_sem=recv,
            device_id=(target, target_core),
            device_id_type=mesh_id,
        )

    def slice_copy(op, n, source, landing):
        return remote(
            source.at[n // mp], landing.at[me], ssem.at[op], rsem.at[op],
            core * per_core + n // mp, lax.rem(n, mp),
        )

    def is_self(n):
        return (core * per_core + n // mp == me) & (lax.rem(n, mp) == core)

    def slice_start(op, source, landing):
        @pl.loop(0, dp)
        def _(n):
            @pl.when(jnp.logical_not(is_self(n)))
            def _():
                slice_copy(op, n, source, landing).start()

        @pl.when(at_home)
        def _():
            landing[me] = source[slot]

    def arrived(op, landing, count):
        some = landing.at[pl.ds(0, count)]
        remote(some, some, ssem.at[op], rsem.at[op], me, other).wait_recv()

    def departed(op, landing, count):
        some = landing.at[pl.ds(0, count)]
        remote(some, some, ssem.at[op], rsem.at[op], me, other).wait_send()

    def by_home(wait, op, landing, count):
        @pl.when(at_home)
        def _():
            wait(op, landing, count - 1)

        @pl.when(jnp.logical_not(at_home))
        def _():
            wait(op, landing, count)

    def dp_copy(op, k, source, landing):
        target = lax.rem(me + k, dp)
        return remote(
            source(target), landing.at[me], ssem.at[op], rsem.at[op], target, core
        )

    def dp_start(op, source, landing):
        @pl.loop(1, dp, unroll=True)
        def _(k):
            dp_copy(op, k, source, landing).start()

    def dp_wait(op, source, landing):
        arrived(op, landing, dp - 1)

    def mp_copy(op, source, landing):
        return remote(source, landing, msend.at[op], mrecv.at[op], me, other)

    def total_of(landing):
        total = landing[0].astype(f32)
        for j in range(1, dp):
            total = total + landing[j].astype(f32)
        return total

    emb_args = (EMB, es, emb_land)
    slice_start(*emb_args)

    local_copies[0].wait()
    last = [jnp.clip(len_ref[b] - 1, 0, seq_len - 1) + b * seq_len for b in range(subs)]
    one_row = lax.broadcasted_iota(jnp.int32, (8, rows), 0)
    one_col = lax.broadcasted_iota(jnp.int32, (8, rows), 1)
    picked_rows = jnp.zeros((8, rows), f32)
    for b in range(subs):
        picked_rows = jnp.where((one_row == b) & (one_col == last[b]), 1.0, picked_rows)
    last_tokens = plain_product(picked_rows.astype(bf16), xg[core])[:subs]
    xs, x_land = r["xs"], r["x_land"]
    for c in range(per_core):
        xs[c] = last_tokens[:, c * dq : (c + 1) * dq]
    xs_args = (XS, xs, x_land)
    slice_start(*xs_args)
    x_copy = mp_copy(M_X, xg.at[core], xg.at[core])
    x_copy.start()

    by_home(arrived, EMB, emb_land, dp)
    emb = emb_land[...].astype(f32)
    queries = emb[:, :local_rows].reshape(batch, dq).astype(bf16)
    items = emb[:, local_rows:].reshape(batch, dq).astype(bf16)
    sc, sc_land = r["sc"], r["sc_land"]
    sc[...] = final_product(queries, items).reshape(dp, local_rows, batch)
    sc_args = (SC, lambda t: sc.at[t], sc_land)
    dp_start(*sc_args)
    sc_land[me] = sc[me]

    by_home(arrived, XS, x_land, dp)
    x_rows = r["x_rows"]
    for j in range(dp):
        x_rows[j * subs : (j + 1) * subs, :] = x_land[j]
    local_copies[1].wait()
    part_q, land_q = r["part_q"], r["land_q"]
    query_part = plain_product(x_rows[...].astype(bf16), wq[...])
    for j in range(dp):
        part_q[j] = query_part[j * subs : (j + 1) * subs]

    columns = lax.broadcasted_iota(jnp.int32, (local_rows, batch), 1)
    row_ids = lax.broadcasted_iota(jnp.int32, (local_rows, batch), 0)
    hard_count = jnp.zeros((local_rows, batch), f32)
    target = jnp.zeros((local_rows, batch), f32)
    for i in range(local_rows):
        for h in range(hard_ref.shape[0]):
            hit = (row_ids == i) & (columns == hard_ref[h, i])
            hard_count = hard_count + jnp.where(hit, 1.0, 0.0)
        target = jnp.where((row_ids == i) & (columns == pair_ref[i]), 1.0, target)
    dp_wait(*sc_args)
    logits = total_of(sc_land) * INV_TEMP + HARD_NEGATIVE_ADD * hard_count
    row_top = jnp.max(logits, axis=1, keepdims=True)
    log_total = row_top + jnp.log(jnp.sum(jnp.exp(logits - row_top), axis=1, keepdims=True))
    picked = jnp.sum(target * logits, axis=1, keepdims=True)
    loss_part = jnp.sum(log_total - picked, axis=0, keepdims=True)
    residual = (jnp.exp(logits - log_total) - target).astype(bf16).astype(f32)
    res_own, res_land = r["res_own"], r["res_land"]
    res_own[...] = residual
    res_args = (RES, lambda t: res_own, res_land)
    dp_start(*res_args)
    res_land[me] = residual
    q_args = (QP, lambda t: part_q.at[t], land_q)
    dp_start(*q_args)
    land_q[me] = part_q[me]

    for i in (2, 3, 5, 6):
        local_copies[i].wait()

    def project(which):
        spot = pl.ds(pl.multiple_of(which * feats, feats), feats)
        block = xg[which]
        return plain_product(block, wkv[spot, :]), final_product(block, down[:, spot])

    acc, acc_low = r["acc"], r["acc_low"]
    acc[...], acc_low[...] = project(core)

    dp_wait(*res_args)
    res = res_land[...].reshape(batch, batch)
    query_grad = plain_product(res.astype(bf16), items) * INV_TEMP
    item_grad = (plain_product(res.T.astype(bf16), queries) * INV_TEMP).astype(bf16).astype(f32)
    item_slabs = item_grad.reshape(dp, local_rows, dq)
    cot_rows = r["cot_rows"]
    for j in range(dp):
        cot_rows[j * subs : (j + 1) * subs, :] = item_slabs[j, :subs]
    local_copies[4].wait()
    part_a, land_a = r["part_a"], r["land_a"]
    grad_part = final_product(cot_rows[...].astype(bf16), wo[...])
    for j in range(dp):
        part_a[j] = grad_part[j * subs : (j + 1) * subs]
    a_args = (AP, lambda t: part_a.at[t], land_a)
    dp_start(*a_args)
    land_a[me] = part_a[me]
    gs, g_land = r["gs"], r["g_land"]
    gs[...] = jnp.concatenate(
        [query_grad.reshape(dp, local_rows, dq), item_slabs], axis=1
    ).astype(bf16)

    def back_copy(k):
        to = lax.rem(me + k, dp)
        return remote(gs.at[to], g_land.at[slot], ssem.at[GB], rsem.at[GB], to, core)

    @pl.when(at_home)
    def _():
        @pl.loop(1, dp)
        def _(k):
            back_copy(k).start()

        g_land[slot] = gs[me]

    x_copy.wait()
    more, more_low = project(other)
    low = (acc_low[...] + more_low).astype(bf16)
    low_key, low_value = low[:, :rank], low[:, rank:]
    key_part, value_part = acc[:, :kw] + more[:, :kw], acc[:, kw:] + more[:, kw:]
    keys = (key_part + ADAPTER_SCALE * plain_product(low_key, kup_ref[...])).astype(bf16)
    values = (value_part + ADAPTER_SCALE * plain_product(low_value, vup_ref[...])).astype(bf16)

    heads = qw // HEAD_DIM
    group_size = HEADS // KV_HEADS
    score_scale = 1.0 / math.sqrt(HEAD_DIM)

    def spread(flat, blocks):
        blocks[...] = jnp.zeros_like(blocks)
        for b in range(subs):
            for h in range(heads):
                kv = h // group_size * HEAD_DIM
                blocks[b * heads + h : b * heads + h + 1, kv : kv + HEAD_DIM] = flat[
                    b : b + 1, h * HEAD_DIM : (h + 1) * HEAD_DIM
                ]
        return blocks[...].astype(bf16)

    dp_wait(*q_args)
    r["flat_q"][...] = total_of(land_q).astype(bf16).astype(f32)
    q_half = spread(r["flat_q"], r["q_blk"])
    raw = final_product(q_half, keys) * score_scale
    head_rows = lax.broadcasted_iota(jnp.int32, raw.shape, 0)
    token_ids = lax.broadcasted_iota(jnp.int32, raw.shape, 1)
    live = jnp.zeros(raw.shape, jnp.bool_)
    for b in range(subs):
        mine = (head_rows >= b * heads) & (head_rows < (b + 1) * heads)
        live = live | (mine & (token_ids >= b * seq_len) & (token_ids <= last[b]))
    raw = jnp.where(live, raw, -jnp.inf)
    weights = jnp.exp(raw - jnp.max(raw, axis=1, keepdims=True))
    probs = weights / jnp.sum(weights, axis=1, keepdims=True)
    dp_wait(*a_args)
    r["flat_a"][...] = total_of(land_a).astype(bf16).astype(f32)
    g_half = spread(r["flat_a"], r["g_blk"])
    prob_grad = final_product(g_half, values)
    score_grad = (
        probs * (prob_grad - jnp.sum(probs * prob_grad, axis=1, keepdims=True)) * score_scale
    ).astype(bf16)

    key_delta = first_product(score_grad, q_half).astype(bf16)
    value_delta = first_product(probs.astype(bf16), g_half).astype(bf16)
    coef = jnp.concatenate(
        [final_product(key_delta, kup_ref[...]), final_product(value_delta, vup_ref[...])], axis=1
    ).astype(bf16)
    coef_g = r["coef_g"]
    coef_g[core] = coef
    coef_copy = mp_copy(M_COEF, coef_g.at[core], coef_g.at[core])
    coef_copy.start()

    query_delta = plain_product(score_grad, keys)
    qd_f, qd_own, qd_all = r["qd_f"], r["qd_own"], r["qd_all"]
    blocks = qw // dq
    in_block = dq // HEAD_DIM
    for b in range(subs):
        for h in range(heads):
            kv = h // group_size * HEAD_DIM
            spot = b * blocks + h // in_block
            lane = h % in_block * HEAD_DIM
            qd_f[spot : spot + 1, lane : lane + HEAD_DIM] = query_delta[
                b * heads + h : b * heads + h + 1, kv : kv + HEAD_DIM
            ]
    qd_own[...] = qd_f[...].astype(bf16)
    qd_args = (QD, lambda t: qd_own, qd_all)
    dp_start(*qd_args)
    qd_all[me] = qd_own[...]

    dn, dn_land, dn_all = r["dn"], r["dn_land"], r["dn_all"]
    up_grad = ADAPTER_SCALE * jnp.concatenate(
        [first_product(low_key, key_delta), first_product(low_value, value_delta)], axis=0
    )
    lane_groups = up_grad.shape[1] // 128
    cols = feats // dp
    own_down = first_product(coef, xg[core])
    for j in range(dp):
        top = j // lane_groups * 8
        lane = j % lane_groups * 128
        up_slab = up_grad[top : top + 8, lane : lane + 128]
        dn[j, 2 * rank :, :] = jnp.concatenate([up_slab, jnp.zeros_like(up_slab)], 0).astype(bf16)
    coef_copy.wait()
    down_part = ADAPTER_SCALE * (own_down + first_product(coef_g[other], xg[core]))
    for j in range(dp):
        dn[j, : 2 * rank, :] = down_part[:, j * cols : (j + 1) * cols].astype(bf16)
    dn_args = (DN, lambda t: dn.at[t], dn_land)
    dp_start(*dn_args)
    dn_land[me] = dn[me]

    pacc, pbuf, p_land, last_f = r["pacc"], r["pbuf"], r["p_land"], r["last_f"]
    deltas = jnp.concatenate([key_delta, value_delta], axis=1)

    def portion(which, place, finish):
        @pl.loop(0, tiles)
        def _(t):
            cols = pl.ds(pl.multiple_of(t * TILE, TILE), TILE)
            spot = pl.ds(pl.multiple_of(which * feats + t * TILE, TILE), TILE)
            pacc[...] = final_product(deltas, wkv[spot, :]) + ADAPTER_SCALE * plain_product(
                coef, down[:, spot]
            )
            for b in range(subs):
                last_f[place, b : b + 1, cols] = pacc[pl.ds(last[b], 1), :]
            finish(cols, pacc[...].astype(bf16))

    def to_other(cols, share):
        pbuf[:, cols] = share

    portion(other, 1, to_other)
    part_copy = mp_copy(M_PART, pbuf, p_land)
    part_copy.start()

    dp_wait(*qd_args)
    changes = qd_all[...].reshape(dp * subs * blocks, dq)
    block_ids = lax.rem(lax.broadcasted_iota(jnp.int32, (dp * subs * blocks, dq), 0), blocks)
    last_part = jnp.zeros((dp * subs * blocks, dq), f32)
    for c in range(blocks):
        term = final_product(changes, wq[:, c * dq : (c + 1) * dq])
        last_part = jnp.where(block_ids == c, term, last_part)
    last_part = jnp.sum(last_part.reshape(dp * subs, blocks, dq), axis=1)
    lp, lp_land = r["lp"], r["lp_land"]
    for j in range(dp):
        lp[j, :subs] = last_part[j * subs : (j + 1) * subs]
        lp[j, subs:] = jnp.broadcast_to(loss_part, (lp.shape[1] - subs, dq))
    lp_args = (LP, lambda t: lp.at[t], lp_land)
    dp_start(*lp_args)
    lp_land[me] = lp[me]

    dp_wait(*dn_args)
    dn_all[core, me] = total_of(dn_land).astype(bf16)
    dng_args = (DNG, lambda t: dn_all.at[core, me], dn_all.at[core])
    dp_start(*dng_args)

    part_copy.wait()

    def to_sum(cols, share):
        r["input_sum"][:, cols] = (share.astype(f32) + p_land[:, cols].astype(f32)).astype(bf16)

    portion(core, 0, to_sum)

    by_home(arrived, GB, g_land, per_core)

    dp_wait(*lp_args)
    last_total, last_send, last_land = r["last_total"], r["last_send"], r["last_land"]
    loss = lp_land[0, subs : subs + 1, 0:1]
    for j in range(1, dp):
        loss = loss + lp_land[j, subs : subs + 1, 0:1]
    r["loss"][...] = loss / batch
    for which in range(mp):
        for c in range(per_core):
            last_total[which, :, c * dq : (c + 1) * dq] = lp_land[which * per_core + c, :subs]
    last_send[...] = (last_f[1] + last_total[other]).astype(bf16).astype(f32)
    last_copy = mp_copy(M_LAST, last_send, last_land)
    last_copy.start()
    dp_wait(*dng_args)
    down_copy = mp_copy(M_DN, dn_all.at[core], dn_all.at[core])
    down_copy.start()

    own_last = (last_f[0] + last_total[core]).astype(bf16).astype(f32)
    last_copy.wait()
    r["last_sum"][...] = own_last + last_land[...]
    for j in range(dp):
        r["up_all"][j] = dn_all[core, j, 2 * rank :, :]
    down_copy.wait()

    by_home(departed, EMB, emb_land, dp)
    by_home(departed, XS, x_land, dp)

    @pl.when(at_home)
    def _():
        departed(GB, gs, dp - 1)

    for op, _, landing in (sc_args, res_args, q_args, a_args, qd_args, lp_args, dn_args, dng_args):
        departed(op, landing, dp - 1)


def result_kernel(
    rank, len_ref, loss_sum, g_land, input_sum, last_sum, dn_all, up_all,
    loss, q_grad, item_grad, input_grad, key_down, value_down, key_up, value_up,
):
    f32, bf16 = jnp.float32, jnp.bfloat16
    mp, dp, _, cols = dn_all.shape
    per_core, group_rows, dq = g_land.shape
    local_rows = group_rows // 2
    subs, feats = last_sum.shape
    rows = input_sum.shape[0]
    seq_len = rows // subs
    loss[...] = loss_sum[...]
    ids = lax.broadcasted_iota(jnp.int32, (rows, dq), 0)
    for c in range(per_core):
        span = slice(c * dq, (c + 1) * dq)
        slab = g_land[c].astype(f32)
        q_grad[:, span] = slab[:local_rows].astype(bf16)
        item_grad[:, span] = slab[local_rows:].astype(bf16)
        ends = last_sum[:, span] + slab[local_rows : local_rows + subs]
        tokens = input_sum[:, span].astype(f32)
        for b in range(subs):
            last = jnp.clip(len_ref[b] - 1, 0, seq_len - 1) + b * seq_len
            tokens = jnp.where(ids == last, ends[b : b + 1], tokens)
        input_grad[:, span] = tokens.astype(bf16)
    lane_groups = key_up.shape[1] // 128
    for j in range(dp):
        top = j // lane_groups * 8
        lane = j % lane_groups * 128
        out = key_up if top < rank else value_up
        slab = up_all[j].astype(f32)
        out[top % rank : top % rank + 8, lane : lane + 128] = slab[:8]
    for which in range(mp):
        for j in range(dp):
            span = slice(which * feats + j * cols, which * feats + (j + 1) * cols)
            slab = dn_all[which, j, : 2 * rank, :].astype(f32)
            key_down[:, span] = slab[:rank]
            value_down[:, span] = slab[rank:]


def fused_local(
    query_emb, item_emb, pair_index, hard_index, hidden_in, lengths, w_query, key_weight_matrix,
    value_weight_matrix, w_out, key_down_matrix, key_up_matrix, value_down, value_up_matrix,
):
    dp, mp = lax.axis_size("dp"), lax.axis_size("mp")
    local_rows, feats = query_emb.shape
    subs, _, seq_len, _ = hidden_in.shape
    rows = subs * seq_len
    rank, kw = key_up_matrix.shape
    dq, qw = w_query.shape
    width = feats * mp
    heads = qw // HEAD_DIM
    batch = dp * local_rows
    per_core = dp // mp
    blocks = qw // dq
    slab = 2 * rank + 16
    f32, bf16 = jnp.float32, jnp.bfloat16
    vmem, hbm = pl.BlockSpec(memory_space=pltpu.VMEM), pl.BlockSpec(memory_space=pl.ANY)
    smem = pl.BlockSpec(memory_space=pltpu.SMEM)
    inputs = {
        "lengths": (lengths[:, 0], smem),
        "pair": (pair_index, smem),
        "hard": (hard_index.T, smem),
        "q": (query_emb, vmem),
        "item": (item_emb, vmem),
        "x": (hidden_in.reshape(rows, feats), hbm),
        "wq_hbm": (w_query, hbm),
        "wk_hbm": (key_weight_matrix, hbm),
        "wv_hbm": (value_weight_matrix, hbm),
        "wo_hbm": (w_out, hbm),
        "kdown": (key_down_matrix.T, hbm),
        "vdown": (value_down.T, hbm),
        "kup": (key_up_matrix, vmem),
        "vup": (value_up_matrix, vmem),
    }
    middle = {
        "loss": ((1, 1), f32),
        "g_land": ((per_core, 2 * local_rows, dq), bf16),
        "input_sum": ((rows, feats), bf16),
        "last_sum": ((subs, feats), f32),
        "dn_all": ((mp, dp, slab, feats // dp), bf16),
        "up_all": ((dp, 16, 128), bf16),
    }
    outputs = (
        ((1, 1), f32),
        ((local_rows, feats), bf16),
        ((local_rows, feats), bf16),
        ((rows, feats), bf16),
        ((rank, width), f32),
        ((rank, width), f32),
        ((rank, kw), f32),
        ((rank, kw), f32),
    )
    scratch = {
        "es": ((per_core, 2 * local_rows, dq), bf16),
        "emb_land": ((dp, 2 * local_rows, dq), bf16),
        "xs": ((per_core, subs, dq), f32),
        "x_land": ((dp, subs, dq), f32),
        "x_rows": ((dp * subs, dq), f32),
        "sc": ((dp, local_rows, batch), f32),
        "sc_land": ((dp, local_rows, batch), f32),
        "res_own": ((local_rows, batch), f32),
        "res_land": ((dp, local_rows, batch), f32),
        "part_q": ((dp, subs, qw), f32),
        "land_q": ((dp, subs, qw), f32),
        "cot_rows": ((dp * subs, dq), f32),
        "part_a": ((dp, subs, qw), f32),
        "land_a": ((dp, subs, qw), f32),
        "gs": ((dp, 2 * local_rows, dq), bf16),
        "xg": ((mp, rows, feats), bf16),
        "wq": ((dq, qw), bf16),
        "wkv": ((width, 2 * kw), bf16),
        "wo": ((qw, dq), bf16),
        "down": ((2 * rank, width), bf16),
        "acc": ((rows, 2 * kw), f32),
        "acc_low": ((rows, 2 * rank), f32),
        "q_blk": ((subs * heads, kw), f32),
        "g_blk": ((subs * heads, kw), f32),
        "flat_q": ((subs, qw), f32),
        "flat_a": ((subs, qw), f32),
        "qd_f": ((subs * blocks, dq), f32),
        "qd_own": ((subs * blocks, dq), bf16),
        "qd_all": ((dp, subs * blocks, dq), bf16),
        "lp": ((dp, 2 * subs, dq), f32),
        "lp_land": ((dp, 2 * subs, dq), f32),
        "coef_g": ((mp, rows, 2 * rank), bf16),
        "pacc": ((rows, TILE), f32),
        "pbuf": ((rows, feats), bf16),
        "p_land": ((rows, feats), bf16),
        "last_f": ((2, subs, feats), f32),
        "last_total": ((mp, subs, feats), f32),
        "last_send": ((subs, feats), f32),
        "last_land": ((subs, feats), f32),
        "dn": ((dp, slab, feats // dp), bf16),
        "dn_land": ((dp, slab, feats // dp), bf16),
    }
    sems = {"ssem": (11,), "rsem": (11,), "msend": (5,), "mrecv": (5,), "csem": (7,)}
    names = (*inputs, *middle, *scratch, *sems)
    parts = pl.pallas_call(
        functools.partial(step_kernel, dp, mp, subs, rank, names),
        out_shape=tuple(jax.ShapeDtypeStruct(s, t) for s, t in middle.values()),
        in_specs=[spec for _, spec in inputs.values()],
        out_specs=(vmem,) * len(middle),
        scratch_shapes=[pltpu.VMEM(s, t) for s, t in scratch.values()]
        + [pltpu.SemaphoreType.DMA(s) for s in sems.values()],
        compiler_params=pltpu.CompilerParams(
            collective_id=0, has_side_effects=True, vmem_limit_bytes=60 * 1024 * 1024
        ),
    )(*(value for value, _ in inputs.values()))
    out = pl.pallas_call(
        functools.partial(result_kernel, rank),
        out_shape=tuple(jax.ShapeDtypeStruct(s, t) for s, t in outputs),
        in_specs=[smem] + [vmem] * len(middle),
        out_specs=(vmem,) * len(outputs),
        compiler_params=pltpu.CompilerParams(vmem_limit_bytes=32 * 1024 * 1024),
    )(lengths[:, 0], *parts)
    loss, query_grad, item_grad, input_grad, key_down, value_down_grad, key_up, value_up = out
    return (
        loss[0, 0],
        query_grad,
        item_grad,
        input_grad.reshape(hidden_in.shape),
        key_down.T,
        value_down_grad.T,
        key_up,
        value_up,
    )


def solution(mesh):
    in_specs = (
        P("dp", "mp"),
        P("dp", "mp"),
        P("dp"),
        P("dp", None),
        P(None, "dp", None, "mp"),
        P(None, "dp"),
        P("dp", "mp"),
        P(None, "mp"),
        P(None, "mp"),
        P("mp", "dp"),
        P(),
        P(None, "mp"),
        P(),
        P(None, "mp"),
    )
    out_specs = (
        P(),
        P("dp", "mp"),
        P("dp", "mp"),
        P(None, "dp", None, "mp"),
        P(),
        P(),
        P(None, "mp"),
        P(None, "mp"),
    )
    small = mesh.shape["mp"] == 2 and mesh.shape["dp"] == 16
    body = fused_local if small else local
    return jax.shard_map(body, mesh=mesh, in_specs=in_specs, out_specs=out_specs, check_vma=False)
```

```python
import functools
import math

import jax
import jax.numpy as jnp
from jax import lax
from jax.experimental import pallas as pl
from jax.experimental.pallas import tpu as pltpu
from jax.sharding import PartitionSpec as P

HEADS = 32
KV_HEADS = 8
HEAD_DIM = 128


INV_TEMP = 50.0
HARD_NEGATIVE_ADD = 4.0
ADAPTER_SCALE = 2.0


def final_product(left_side, right_side):
    return lax.dot_general(
        left_side, right_side, (((1,), (1,)), ((), ())), preferred_element_type=jnp.float32
    )


def first_product(left_side, right_side):
    return lax.dot_general(
        left_side, right_side, (((0,), (0,)), ((), ())), preferred_element_type=jnp.float32
    )


def local(
    query_emb,
    item_emb,
    pair_index,
    hard_index,
    hidden_in,
    lengths,
    w_query,
    key_weight_matrix,
    value_weight_matrix,
    w_out,
    key_down_matrix,
    key_up_matrix,
    value_down,
    value_up_matrix,
):
    dp_count = lax.axis_size("dp")
    local_rows = query_emb.shape[0]
    batch_size = local_rows * dp_count
    items_all = lax.all_gather(item_emb, "dp", axis=0, tiled=True)
    partial_scores = final_product(query_emb, items_all)
    pair_scores = lax.psum(partial_scores, "mp") * INV_TEMP
    columns = jnp.arange(batch_size, dtype=jnp.int32)
    hard_negative_count = jnp.sum(
        (hard_index[:, :, None] == columns[None, None, :]).astype(jnp.float32), axis=1
    )
    score_logits = pair_scores + HARD_NEGATIVE_ADD * hard_negative_count
    row_top = jnp.max(score_logits, axis=1, keepdims=True)
    log_total = row_top[:, 0] + jnp.log(jnp.sum(jnp.exp(score_logits - row_top), axis=1))
    target = (pair_index[:, None] == columns[None, :]).astype(jnp.float32)
    picked = jnp.sum(target * score_logits, axis=1)
    loss_part = jnp.sum(log_total - picked)
    residual = (jnp.exp(score_logits - log_total[:, None]) - target).astype(jnp.bfloat16)
    query_grad = (
        jnp.dot(residual, items_all, preferred_element_type=jnp.float32) * INV_TEMP
    ).astype(jnp.bfloat16)
    item_grad = lax.psum_scatter(
        first_product(residual, query_emb) * INV_TEMP, "dp", scatter_dimension=0, tiled=True
    ).astype(jnp.bfloat16)
    sub_count = hidden_in.shape[0]
    seq_len = hidden_in.shape[2]
    full_rows = lax.all_gather(hidden_in, "mp", axis=3, tiled=True)
    model_width = full_rows.shape[3]
    token_inputs = full_rows.reshape(sub_count * seq_len, model_width)
    seq_lengths = lengths[:, 0]
    last_rows = jnp.arange(sub_count, dtype=jnp.int32) * seq_len + seq_lengths - 1
    last_tokens = jnp.take(token_inputs, last_rows, axis=0)
    cot_local = item_grad[:sub_count]
    cot_full = lax.all_gather(cot_local, "mp", axis=1, tiled=True)
    adapter_rank = key_down_matrix.shape[1]
    down_both = jnp.concatenate([key_down_matrix, value_down], axis=1)
    reduced_pair = jnp.dot(token_inputs, down_both, preferred_element_type=jnp.float32).astype(
        jnp.bfloat16
    )
    reduced_key = reduced_pair[:, :adapter_rank]
    reduced_value = reduced_pair[:, adapter_rank:]
    key_rows = (
        jnp.dot(token_inputs, key_weight_matrix, preferred_element_type=jnp.float32)
        + ADAPTER_SCALE * jnp.dot(reduced_key, key_up_matrix, preferred_element_type=jnp.float32)
    ).astype(jnp.bfloat16)
    value_rows = (
        jnp.dot(token_inputs, value_weight_matrix, preferred_element_type=jnp.float32)
        + ADAPTER_SCALE
        * jnp.dot(reduced_value, value_up_matrix, preferred_element_type=jnp.float32)
    ).astype(jnp.bfloat16)
    query_width = w_query.shape[1]
    wq_full, wo_full = (
        lax.all_gather(w_query, "dp", axis=0, tiled=True),
        lax.all_gather(w_out, "dp", axis=1, tiled=True),
    )
    query = jnp.dot(last_tokens, wq_full, preferred_element_type=jnp.float32).astype(jnp.bfloat16)
    attn_grad = final_product(cot_full, wo_full).astype(jnp.bfloat16)
    group_size = HEADS // KV_HEADS
    kv_local = key_rows.shape[1] // HEAD_DIM
    score_scale = 1.0 / math.sqrt(HEAD_DIM)
    q_heads = query.reshape(sub_count, kv_local, group_size, HEAD_DIM)
    k_heads = key_rows.reshape(sub_count, seq_len, kv_local, HEAD_DIM)
    v_heads = value_rows.reshape(sub_count, seq_len, kv_local, HEAD_DIM)
    raw_scores = (
        jnp.einsum("bkgd,bjkd->bkgj", q_heads, k_heads, preferred_element_type=jnp.float32)
        * score_scale
    )
    live_mask = jnp.arange(seq_len, dtype=jnp.int32)[None, :] < seq_lengths[:, None]
    raw_scores = jnp.where(live_mask[:, None, None, :], raw_scores, -jnp.inf)
    row_peak = jnp.max(raw_scores, axis=-1, keepdims=True)
    weights = jnp.exp(raw_scores - row_peak)
    softmax_probs = weights / jnp.sum(weights, axis=-1, keepdims=True)
    prob_half = softmax_probs.astype(jnp.bfloat16)
    grad_heads = attn_grad.reshape(sub_count, kv_local, group_size, HEAD_DIM)
    prob_grad = jnp.einsum(
        "bkgd,bjkd->bkgj", grad_heads, v_heads, preferred_element_type=jnp.float32
    )
    score_grad = (
        softmax_probs
        * (prob_grad - jnp.sum(softmax_probs * prob_grad, axis=-1, keepdims=True))
        * score_scale
    ).astype(jnp.bfloat16)
    query_delta = (
        jnp.einsum("bkgj,bjkd->bkgd", score_grad, k_heads, preferred_element_type=jnp.float32)
        .astype(jnp.bfloat16)
        .reshape(sub_count, query_width)
    )
    key_adapter_change = (
        jnp.einsum("bkgj,bkgd->bjkd", score_grad, q_heads, preferred_element_type=jnp.float32)
        .astype(jnp.bfloat16)
        .reshape(sub_count * seq_len, kv_local * HEAD_DIM)
    )
    value_adapter_change = (
        jnp.einsum("bkgj,bkgd->bjkd", prob_half, grad_heads, preferred_element_type=jnp.float32)
        .astype(jnp.bfloat16)
        .reshape(sub_count * seq_len, kv_local * HEAD_DIM)
    )
    last_part = final_product(query_delta, wq_full)
    key_coefficient = final_product(key_adapter_change, key_up_matrix).astype(jnp.bfloat16)
    value_coefficient = final_product(value_adapter_change, value_up_matrix).astype(jnp.bfloat16)
    input_portion = final_product(key_adapter_change, key_weight_matrix) + final_product(
        value_adapter_change, value_weight_matrix
    )
    input_portion = input_portion + ADAPTER_SCALE * (
        final_product(key_coefficient, key_down_matrix)
        + final_product(value_coefficient, value_down)
    )
    input_portion = input_portion.at[last_rows].add(last_part)
    input_sum = lax.psum_scatter(
        input_portion.astype(jnp.bfloat16), "mp", scatter_dimension=1, tiled=True
    ).astype(jnp.float32)
    input_sum = input_sum.at[last_rows].add(cot_local.astype(jnp.float32))
    input_grad = input_sum.astype(jnp.bfloat16).reshape(hidden_in.shape)
    key_down_grad, value_down_grad = lax.psum(
        (
            ADAPTER_SCALE * first_product(token_inputs, key_coefficient),
            ADAPTER_SCALE * first_product(token_inputs, value_coefficient),
        ),
        ("dp", "mp"),
    )
    total_loss, key_up_grad, value_up_grad = lax.psum(
        (
            loss_part,
            ADAPTER_SCALE * first_product(reduced_key, key_adapter_change),
            ADAPTER_SCALE * first_product(reduced_value, value_adapter_change),
        ),
        "dp",
    )
    mean_loss = total_loss / batch_size
    return (
        mean_loss,
        query_grad,
        item_grad,
        input_grad,
        key_down_grad,
        value_down_grad,
        key_up_grad,
        value_up_grad,
    )


TILE = 1024
PLANE = 4
EMB, XS, SC, RES, QP, QZ, AP, AZ, GB, QD, LP, DN, DZ, DNG = range(14)
M_X, M_COEF, M_PART, M_LAST, M_DN = range(5)


def plain_product(left_side, right_side):
    return jnp.dot(left_side, right_side, preferred_element_type=jnp.float32)


def step_kernel(
    dp, mp, subs, rank, names, *refs,
):
    r = dict(zip(names, refs, strict=True))
    len_ref, pair_ref, hard_ref = r["lengths"], r["pair"], r["hard"]
    q_ref, item_ref, x_hbm, kup_ref, vup_ref = r["q"], r["item"], r["x"], r["kup"], r["vup"]
    xg, wq, wkv, wo, down = r["xg"], r["wq"], r["wkv"], r["wo"], r["down"]
    ssem, rsem, msend, mrecv, csem = r["ssem"], r["rsem"], r["msend"], r["mrecv"], r["csem"]
    me = lax.axis_index("dp")
    core = lax.axis_index("mp")
    other = 1 - core
    rows, feats = x_hbm.shape
    seq_len = rows // subs
    local_rows = q_ref.shape[0]
    batch = dp * local_rows
    dq, qw = wq.shape
    kw = wkv.shape[1] // 2
    tiles = feats // TILE
    per_core = dp // mp
    home = me // per_core
    slot = lax.rem(me, per_core)
    at_home = core == home
    mesh_id = pl.DeviceIdType.MESH
    f32, bf16 = jnp.float32, jnp.bfloat16

    local_copies = [
        pltpu.make_async_copy(src, dst, csem.at[i])
        for i, (src, dst) in enumerate(
            (
                (x_hbm, xg.at[core]),
                (r["wq_hbm"], wq),
                (r["wk_hbm"], wkv.at[:, pl.ds(0, kw)]),
                (r["wv_hbm"], wkv.at[:, pl.ds(kw, kw)]),
                (r["wo_hbm"], wo),
                (r["kdown"], down.at[pl.ds(0, rank)]),
                (r["vdown"], down.at[pl.ds(rank, rank)]),
            )
        )
    ]
    for copy in local_copies:
        copy.start()

    barrier = pltpu.get_barrier_semaphore()

    @pl.loop(1, dp * mp)
    def _(n):
        flat = lax.rem(me * mp + core + n, dp * mp)
        pl.semaphore_signal(
            barrier, inc=1, device_id=(flat // mp, lax.rem(flat, mp)), device_id_type=mesh_id
        )

    es, emb_land = r["es"], r["emb_land"]
    both = jnp.concatenate([q_ref[...].astype(f32), item_ref[...].astype(f32)], axis=0)
    for c in range(per_core):
        es[c] = both[:, c * dq : (c + 1) * dq].astype(bf16)
    pl.semaphore_wait(barrier, dp * mp - 1)

    def remote(source, landing, send, recv, target, target_core):
        return pltpu.make_async_remote_copy(
            src_ref=source,
            dst_ref=landing,
            send_sem=send,
            recv_sem=recv,
            device_id=(target, target_core),
            device_id_type=mesh_id,
        )

    def slice_copy(op, n, source, landing):
        return remote(
            source.at[n // mp], landing.at[me], ssem.at[op], rsem.at[op],
            core * per_core + n // mp, lax.rem(n, mp),
        )

    def is_self(n):
        return (core * per_core + n // mp == me) & (lax.rem(n, mp) == core)

    def slice_start(op, source, landing):
        @pl.loop(0, dp)
        def _(n):
            @pl.when(jnp.logical_not(is_self(n)))
            def _():
                slice_copy(op, n, source, landing).start()

        @pl.when(at_home)
        def _():
            landing[me] = source[slot]

    def arrived(op, landing, count):
        some = landing.at[pl.ds(0, count)]
        remote(some, some, ssem.at[op], rsem.at[op], me, other).wait_recv()

    def departed(op, landing, count):
        some = landing.at[pl.ds(0, count)]
        remote(some, some, ssem.at[op], rsem.at[op], me, other).wait_send()

    def by_home(wait, op, landing, count):
        @pl.when(at_home)
        def _():
            wait(op, landing, count - 1)

        @pl.when(jnp.logical_not(at_home))
        def _():
            wait(op, landing, count)

    def dp_copy(op, k, source, landing):
        target = lax.rem(me + k, dp)
        return remote(
            source(target), landing.at[me], ssem.at[op], rsem.at[op], target, core
        )

    def dp_start(op, source, landing):
        @pl.loop(1, dp, unroll=True)
        def _(k):
            dp_copy(op, k, source, landing).start()

    def dp_wait(op, source, landing):
        arrived(op, landing, dp - 1)

    def mp_copy(op, source, landing):
        return remote(source, landing, msend.at[op], mrecv.at[op], me, other)

    def total_of(landing):
        total = landing[0].astype(f32)
        for j in range(1, landing.shape[0]):
            total = total + landing[j].astype(f32)
        return total

    spot_in_plane, level = lax.rem(me, PLANE), me // PLANE
    levels = dp // PLANE

    def plane_start(op, source, landing):
        for k in range(1, PLANE):
            to = lax.rem(spot_in_plane + k, PLANE)
            remote(
                source.at[to], landing.at[spot_in_plane], ssem.at[op], rsem.at[op],
                level * PLANE + to, core,
            ).start()
        landing[spot_in_plane] = source[spot_in_plane]

    def line_start(op, plane_op, plane_landing, source, landing):
        arrived(plane_op, plane_landing, PLANE - 1)
        source[...] = total_of(plane_landing)
        for k in range(1, levels):
            to = lax.rem(level + k, levels)
            remote(
                source.at[to], landing.at[level], ssem.at[op], rsem.at[op],
                to * PLANE + spot_in_plane, core,
            ).start()
        landing[level] = source[level]

    def line_total(op, landing):
        arrived(op, landing, levels - 1)
        return total_of(landing)

    emb_args = (EMB, es, emb_land)
    slice_start(*emb_args)

    local_copies[0].wait()
    last = [jnp.clip(len_ref[b] - 1, 0, seq_len - 1) + b * seq_len for b in range(subs)]
    one_row = lax.broadcasted_iota(jnp.int32, (8, rows), 0)
    one_col = lax.broadcasted_iota(jnp.int32, (8, rows), 1)
    picked_rows = jnp.zeros((8, rows), f32)
    for b in range(subs):
        picked_rows = jnp.where((one_row == b) & (one_col == last[b]), 1.0, picked_rows)
    last_tokens = plain_product(picked_rows.astype(bf16), xg[core])[:subs]
    xs, x_land = r["xs"], r["x_land"]
    for c in range(per_core):
        xs[c] = last_tokens[:, c * dq : (c + 1) * dq]
    xs_args = (XS, xs, x_land)
    slice_start(*xs_args)
    x_copy = mp_copy(M_X, xg.at[core], xg.at[core])
    x_copy.start()

    by_home(arrived, EMB, emb_land, dp)
    emb = emb_land[...].astype(f32)
    queries = emb[:, :local_rows].reshape(batch, dq).astype(bf16)
    items = emb[:, local_rows:].reshape(batch, dq).astype(bf16)
    sc, sc_land = r["sc"], r["sc_land"]
    sc[...] = final_product(queries, items).reshape(dp, local_rows, batch)
    sc_args = (SC, lambda t: sc.at[t], sc_land)
    dp_start(*sc_args)
    sc_land[me] = sc[me]

    by_home(arrived, XS, x_land, dp)
    x_rows = r["x_rows"]
    for j in range(dp):
        x_rows[j * subs : (j + 1) * subs, :] = x_land[j]
    local_copies[1].wait()
    part_q, plane_q, line_q, land_q = r["part_q"], r["plane_q"], r["line_q"], r["land_q"]
    query_part = plain_product(x_rows[...].astype(bf16), wq[...])
    for j in range(dp):
        part_q[j % PLANE, j // PLANE] = query_part[j * subs : (j + 1) * subs]

    columns = lax.broadcasted_iota(jnp.int32, (local_rows, batch), 1)
    row_ids = lax.broadcasted_iota(jnp.int32, (local_rows, batch), 0)
    hard_count = jnp.zeros((local_rows, batch), f32)
    target = jnp.zeros((local_rows, batch), f32)
    for i in range(local_rows):
        for h in range(hard_ref.shape[0]):
            hit = (row_ids == i) & (columns == hard_ref[h, i])
            hard_count = hard_count + jnp.where(hit, 1.0, 0.0)
        target = jnp.where((row_ids == i) & (columns == pair_ref[i]), 1.0, target)
    dp_wait(*sc_args)
    logits = total_of(sc_land) * INV_TEMP + HARD_NEGATIVE_ADD * hard_count
    row_top = jnp.max(logits, axis=1, keepdims=True)
    log_total = row_top + jnp.log(jnp.sum(jnp.exp(logits - row_top), axis=1, keepdims=True))
    picked = jnp.sum(target * logits, axis=1, keepdims=True)
    loss_part = jnp.sum(log_total - picked, axis=0, keepdims=True)
    residual = (jnp.exp(logits - log_total) - target).astype(bf16).astype(f32)
    res_own, res_land = r["res_own"], r["res_land"]
    res_own[...] = residual
    res_args = (RES, lambda t: res_own, res_land)
    dp_start(*res_args)
    res_land[me] = residual
    plane_start(QP, part_q, plane_q)

    for i in (2, 3, 5, 6):
        local_copies[i].wait()

    def project(which):
        spot = pl.ds(pl.multiple_of(which * feats, feats), feats)
        block = xg[which]
        return plain_product(block, wkv[spot, :]), final_product(block, down[:, spot])

    acc, acc_low = r["acc"], r["acc_low"]
    acc[...], acc_low[...] = project(core)
    line_start(QZ, QP, plane_q, line_q, land_q)

    dp_wait(*res_args)
    res = res_land[...].reshape(batch, batch)
    query_grad = plain_product(res.astype(bf16), items) * INV_TEMP
    item_grad = (plain_product(res.T.astype(bf16), queries) * INV_TEMP).astype(bf16).astype(f32)
    item_slabs = item_grad.reshape(dp, local_rows, dq)
    cot_rows = r["cot_rows"]
    for j in range(dp):
        cot_rows[j * subs : (j + 1) * subs, :] = item_slabs[j, :subs]
    local_copies[4].wait()
    part_a, plane_a, line_a, land_a = r["part_a"], r["plane_a"], r["line_a"], r["land_a"]
    grad_part = final_product(cot_rows[...].astype(bf16), wo[...])
    for j in range(dp):
        part_a[j % PLANE, j // PLANE] = grad_part[j * subs : (j + 1) * subs]
    plane_start(AP, part_a, plane_a)
    gs, g_land = r["gs"], r["g_land"]
    gs[...] = jnp.concatenate(
        [query_grad.reshape(dp, local_rows, dq), item_slabs], axis=1
    ).astype(bf16)

    def back_copy(k):
        to = lax.rem(me + k, dp)
        return remote(gs.at[to], g_land.at[slot], ssem.at[GB], rsem.at[GB], to, core)

    @pl.when(at_home)
    def _():
        @pl.loop(1, dp)
        def _(k):
            back_copy(k).start()

        g_land[slot] = gs[me]

    x_copy.wait()
    more, more_low = project(other)
    line_start(AZ, AP, plane_a, line_a, land_a)
    low = (acc_low[...] + more_low).astype(bf16)
    low_key, low_value = low[:, :rank], low[:, rank:]
    key_part, value_part = acc[:, :kw] + more[:, :kw], acc[:, kw:] + more[:, kw:]
    keys = (key_part + ADAPTER_SCALE * plain_product(low_key, kup_ref[...])).astype(bf16)
    values = (value_part + ADAPTER_SCALE * plain_product(low_value, vup_ref[...])).astype(bf16)

    heads = qw // HEAD_DIM
    group_size = HEADS // KV_HEADS
    score_scale = 1.0 / math.sqrt(HEAD_DIM)

    def spread(flat, blocks):
        blocks[...] = jnp.zeros_like(blocks)
        for b in range(subs):
            for h in range(heads):
                kv = h // group_size * HEAD_DIM
                blocks[b * heads + h : b * heads + h + 1, kv : kv + HEAD_DIM] = flat[
                    b : b + 1, h * HEAD_DIM : (h + 1) * HEAD_DIM
                ]
        return blocks[...].astype(bf16)

    r["flat_q"][...] = line_total(QZ, land_q).astype(bf16).astype(f32)
    q_half = spread(r["flat_q"], r["q_blk"])
    raw = final_product(q_half, keys) * score_scale
    head_rows = lax.broadcasted_iota(jnp.int32, raw.shape, 0)
    token_ids = lax.broadcasted_iota(jnp.int32, raw.shape, 1)
    live = jnp.zeros(raw.shape, jnp.bool_)
    for b in range(subs):
        mine = (head_rows >= b * heads) & (head_rows < (b + 1) * heads)
        live = live | (mine & (token_ids >= b * seq_len) & (token_ids <= last[b]))
    raw = jnp.where(live, raw, -jnp.inf)
    weights = jnp.exp(raw - jnp.max(raw, axis=1, keepdims=True))
    probs = weights / jnp.sum(weights, axis=1, keepdims=True)
    r["flat_a"][...] = line_total(AZ, land_a).astype(bf16).astype(f32)
    g_half = spread(r["flat_a"], r["g_blk"])
    prob_grad = final_product(g_half, values)
    score_grad = (
        probs * (prob_grad - jnp.sum(probs * prob_grad, axis=1, keepdims=True)) * score_scale
    ).astype(bf16)

    key_delta = first_product(score_grad, q_half).astype(bf16)
    value_delta = first_product(probs.astype(bf16), g_half).astype(bf16)
    coef = jnp.concatenate(
        [final_product(key_delta, kup_ref[...]), final_product(value_delta, vup_ref[...])], axis=1
    ).astype(bf16)
    coef_g = r["coef_g"]
    coef_g[core] = coef
    coef_copy = mp_copy(M_COEF, coef_g.at[core], coef_g.at[core])
    coef_copy.start()

    query_delta = plain_product(score_grad, keys)
    qd_f, qd_own, qd_all = r["qd_f"], r["qd_own"], r["qd_all"]
    blocks = qw // dq
    in_block = dq // HEAD_DIM
    for b in range(subs):
        for h in range(heads):
            kv = h // group_size * HEAD_DIM
            spot = b * blocks + h // in_block
            lane = h % in_block * HEAD_DIM
            qd_f[spot : spot + 1, lane : lane + HEAD_DIM] = query_delta[
                b * heads + h : b * heads + h + 1, kv : kv + HEAD_DIM
            ]
    qd_own[...] = qd_f[...].astype(bf16)
    qd_args = (QD, lambda t: qd_own, qd_all)
    dp_start(*qd_args)
    qd_all[me] = qd_own[...]

    dn, dn_plane, dn_line, dn_land = r["dn"], r["dn_plane"], r["dn_line"], r["dn_land"]
    dn_all = r["dn_all"]
    up_grad = ADAPTER_SCALE * jnp.concatenate(
        [first_product(low_key, key_delta), first_product(low_value, value_delta)], axis=0
    )
    lane_groups = up_grad.shape[1] // 128
    cols = feats // dp
    own_down = first_product(coef, xg[core])
    for j in range(dp):
        top = j // lane_groups * 8
        lane = j % lane_groups * 128
        dn[j % PLANE, j // PLANE, 2 * rank :, :] = up_grad[top : top + 8, lane : lane + 128]
    coef_copy.wait()
    down_part = ADAPTER_SCALE * (own_down + first_product(coef_g[other], xg[core]))
    for j in range(dp):
        dn[j % PLANE, j // PLANE, : 2 * rank, :] = down_part[:, j * cols : (j + 1) * cols]
    plane_start(DN, dn, dn_plane)

    pacc, pbuf, p_land, last_f = r["pacc"], r["pbuf"], r["p_land"], r["last_f"]
    deltas = jnp.concatenate([key_delta, value_delta], axis=1)

    def portion(which, place, finish):
        @pl.loop(0, tiles)
        def _(t):
            cols = pl.ds(pl.multiple_of(t * TILE, TILE), TILE)
            spot = pl.ds(pl.multiple_of(which * feats + t * TILE, TILE), TILE)
            pacc[...] = final_product(deltas, wkv[spot, :]) + ADAPTER_SCALE * plain_product(
                coef, down[:, spot]
            )
            for b in range(subs):
                last_f[place, b : b + 1, cols] = pacc[pl.ds(last[b], 1), :]
            finish(cols, pacc[...].astype(bf16))

    def to_other(cols, share):
        pbuf[:, cols] = share

    portion(other, 1, to_other)
    part_copy = mp_copy(M_PART, pbuf, p_land)
    part_copy.start()

    dp_wait(*qd_args)
    changes = qd_all[...].reshape(dp * subs * blocks, dq)
    block_ids = lax.rem(lax.broadcasted_iota(jnp.int32, (dp * subs * blocks, dq), 0), blocks)
    last_part = jnp.zeros((dp * subs * blocks, dq), f32)
    for c in range(blocks):
        term = final_product(changes, wq[:, c * dq : (c + 1) * dq])
        last_part = jnp.where(block_ids == c, term, last_part)
    last_part = jnp.sum(last_part.reshape(dp * subs, blocks, dq), axis=1)
    lp, lp_land = r["lp"], r["lp_land"]
    for j in range(dp):
        lp[j, :subs] = last_part[j * subs : (j + 1) * subs]
        lp[j, subs:] = jnp.broadcast_to(loss_part, (lp.shape[1] - subs, dq))
    lp_args = (LP, lambda t: lp.at[t], lp_land)
    dp_start(*lp_args)
    lp_land[me] = lp[me]
    line_start(DZ, DN, dn_plane, dn_line, dn_land)

    part_copy.wait()

    def to_sum(cols, share):
        r["input_sum"][:, cols] = (share.astype(f32) + p_land[:, cols].astype(f32)).astype(bf16)

    portion(core, 0, to_sum)

    dn_sum = line_total(DZ, dn_land)
    dn_all[core, me] = jnp.concatenate([dn_sum, jnp.zeros((8, cols), f32)], 0).astype(bf16)
    dng_args = (DNG, lambda t: dn_all.at[core, me], dn_all.at[core])
    dp_start(*dng_args)


    by_home(arrived, GB, g_land, per_core)

    dp_wait(*lp_args)
    last_total, last_send, last_land = r["last_total"], r["last_send"], r["last_land"]
    loss = lp_land[0, subs : subs + 1, 0:1]
    for j in range(1, dp):
        loss = loss + lp_land[j, subs : subs + 1, 0:1]
    r["loss"][...] = loss / batch
    for which in range(mp):
        for c in range(per_core):
            last_total[which, :, c * dq : (c + 1) * dq] = lp_land[which * per_core + c, :subs]
    last_send[...] = (last_f[1] + last_total[other]).astype(bf16).astype(f32)
    last_copy = mp_copy(M_LAST, last_send, last_land)
    last_copy.start()
    dp_wait(*dng_args)
    down_copy = mp_copy(M_DN, dn_all.at[core], dn_all.at[core])
    down_copy.start()

    own_last = (last_f[0] + last_total[core]).astype(bf16).astype(f32)
    last_copy.wait()
    r["last_sum"][...] = own_last + last_land[...]
    for j in range(dp):
        r["up_all"][j] = dn_all[core, j, 2 * rank :, :]
    down_copy.wait()

    by_home(departed, EMB, emb_land, dp)
    by_home(departed, XS, x_land, dp)

    @pl.when(at_home)
    def _():
        departed(GB, gs, dp - 1)

    for op, _, landing in (sc_args, res_args, qd_args, lp_args, dng_args):
        departed(op, landing, dp - 1)
    for op, landing in ((QP, plane_q), (AP, plane_a), (DN, dn_plane)):
        departed(op, landing, PLANE - 1)
    for op, landing in ((QZ, land_q), (AZ, land_a), (DZ, dn_land)):
        departed(op, landing, levels - 1)


def result_kernel(
    rank, len_ref, loss_sum, g_land, input_sum, last_sum, dn_all, up_all,
    loss, q_grad, item_grad, input_grad, key_down, value_down, key_up, value_up,
):
    f32, bf16 = jnp.float32, jnp.bfloat16
    mp, dp, _, cols = dn_all.shape
    per_core, group_rows, dq = g_land.shape
    local_rows = group_rows // 2
    subs, feats = last_sum.shape
    rows = input_sum.shape[0]
    seq_len = rows // subs
    loss[...] = loss_sum[...]
    ids = lax.broadcasted_iota(jnp.int32, (rows, dq), 0)
    for c in range(per_core):
        span = slice(c * dq, (c + 1) * dq)
        slab = g_land[c].astype(f32)
        q_grad[:, span] = slab[:local_rows].astype(bf16)
        item_grad[:, span] = slab[local_rows:].astype(bf16)
        ends = last_sum[:, span] + slab[local_rows : local_rows + subs]
        tokens = input_sum[:, span].astype(f32)
        for b in range(subs):
            last = jnp.clip(len_ref[b] - 1, 0, seq_len - 1) + b * seq_len
            tokens = jnp.where(ids == last, ends[b : b + 1], tokens)
        input_grad[:, span] = tokens.astype(bf16)
    lane_groups = key_up.shape[1] // 128
    for j in range(dp):
        top = j // lane_groups * 8
        lane = j % lane_groups * 128
        out = key_up if top < rank else value_up
        slab = up_all[j].astype(f32)
        out[top % rank : top % rank + 8, lane : lane + 128] = slab[:8]
    for which in range(mp):
        for j in range(dp):
            span = slice(which * feats + j * cols, which * feats + (j + 1) * cols)
            slab = dn_all[which, j, : 2 * rank, :].astype(f32)
            key_down[:, span] = slab[:rank]
            value_down[:, span] = slab[rank:]


def fused_local(
    query_emb, item_emb, pair_index, hard_index, hidden_in, lengths, w_query, key_weight_matrix,
    value_weight_matrix, w_out, key_down_matrix, key_up_matrix, value_down, value_up_matrix,
):
    dp, mp = lax.axis_size("dp"), lax.axis_size("mp")
    local_rows, feats = query_emb.shape
    subs, _, seq_len, _ = hidden_in.shape
    rows = subs * seq_len
    rank, kw = key_up_matrix.shape
    dq, qw = w_query.shape
    width = feats * mp
    heads = qw // HEAD_DIM
    batch = dp * local_rows
    per_core = dp // mp
    levels = dp // PLANE
    blocks = qw // dq
    slab = 2 * rank + 16
    f32, bf16 = jnp.float32, jnp.bfloat16
    vmem, hbm = pl.BlockSpec(memory_space=pltpu.VMEM), pl.BlockSpec(memory_space=pl.ANY)
    smem = pl.BlockSpec(memory_space=pltpu.SMEM)
    inputs = {
        "lengths": (lengths[:, 0], smem),
        "pair": (pair_index, smem),
        "hard": (hard_index.T, smem),
        "q": (query_emb, vmem),
        "item": (item_emb, vmem),
        "x": (hidden_in.reshape(rows, feats), hbm),
        "wq_hbm": (w_query, hbm),
        "wk_hbm": (key_weight_matrix, hbm),
        "wv_hbm": (value_weight_matrix, hbm),
        "wo_hbm": (w_out, hbm),
        "kdown": (key_down_matrix.T, hbm),
        "vdown": (value_down.T, hbm),
        "kup": (key_up_matrix, vmem),
        "vup": (value_up_matrix, vmem),
    }
    middle = {
        "loss": ((1, 1), f32),
        "g_land": ((per_core, 2 * local_rows, dq), bf16),
        "input_sum": ((rows, feats), bf16),
        "last_sum": ((subs, feats), f32),
        "dn_all": ((mp, dp, slab, feats // dp), bf16),
        "up_all": ((dp, 16, 128), bf16),
    }
    outputs = (
        ((1, 1), f32),
        ((local_rows, feats), bf16),
        ((local_rows, feats), bf16),
        ((rows, feats), bf16),
        ((rank, width), f32),
        ((rank, width), f32),
        ((rank, kw), f32),
        ((rank, kw), f32),
    )
    scratch = {
        "es": ((per_core, 2 * local_rows, dq), bf16),
        "emb_land": ((dp, 2 * local_rows, dq), bf16),
        "xs": ((per_core, subs, dq), f32),
        "x_land": ((dp, subs, dq), f32),
        "x_rows": ((dp * subs, dq), f32),
        "sc": ((dp, local_rows, batch), f32),
        "sc_land": ((dp, local_rows, batch), f32),
        "res_own": ((local_rows, batch), f32),
        "res_land": ((dp, local_rows, batch), f32),
        "part_q": ((PLANE, levels, subs, qw), f32),
        "plane_q": ((PLANE, levels, subs, qw), f32),
        "line_q": ((levels, subs, qw), f32),
        "land_q": ((levels, subs, qw), f32),
        "cot_rows": ((dp * subs, dq), f32),
        "part_a": ((PLANE, levels, subs, qw), f32),
        "plane_a": ((PLANE, levels, subs, qw), f32),
        "line_a": ((levels, subs, qw), f32),
        "land_a": ((levels, subs, qw), f32),
        "gs": ((dp, 2 * local_rows, dq), bf16),
        "xg": ((mp, rows, feats), bf16),
        "wq": ((dq, qw), bf16),
        "wkv": ((width, 2 * kw), bf16),
        "wo": ((qw, dq), bf16),
        "down": ((2 * rank, width), bf16),
        "acc": ((rows, 2 * kw), f32),
        "acc_low": ((rows, 2 * rank), f32),
        "q_blk": ((subs * heads, kw), f32),
        "g_blk": ((subs * heads, kw), f32),
        "flat_q": ((subs, qw), f32),
        "flat_a": ((subs, qw), f32),
        "qd_f": ((subs * blocks, dq), f32),
        "qd_own": ((subs * blocks, dq), bf16),
        "qd_all": ((dp, subs * blocks, dq), bf16),
        "lp": ((dp, 2 * subs, dq), f32),
        "lp_land": ((dp, 2 * subs, dq), f32),
        "coef_g": ((mp, rows, 2 * rank), bf16),
        "pacc": ((rows, TILE), f32),
        "pbuf": ((rows, feats), bf16),
        "p_land": ((rows, feats), bf16),
        "last_f": ((2, subs, feats), f32),
        "last_total": ((mp, subs, feats), f32),
        "last_send": ((subs, feats), f32),
        "last_land": ((subs, feats), f32),
        "dn": ((PLANE, levels, slab - 8, feats // dp), f32),
        "dn_plane": ((PLANE, levels, slab - 8, feats // dp), f32),
        "dn_line": ((levels, slab - 8, feats // dp), f32),
        "dn_land": ((levels, slab - 8, feats // dp), f32),
    }
    sems = {"ssem": (14,), "rsem": (14,), "msend": (5,), "mrecv": (5,), "csem": (7,)}
    names = (*inputs, *middle, *scratch, *sems)
    parts = pl.pallas_call(
        functools.partial(step_kernel, dp, mp, subs, rank, names),
        out_shape=tuple(jax.ShapeDtypeStruct(s, t) for s, t in middle.values()),
        in_specs=[spec for _, spec in inputs.values()],
        out_specs=(vmem,) * len(middle),
        scratch_shapes=[pltpu.VMEM(s, t) for s, t in scratch.values()]
        + [pltpu.SemaphoreType.DMA(s) for s in sems.values()],
        compiler_params=pltpu.CompilerParams(
            collective_id=0, has_side_effects=True, vmem_limit_bytes=60 * 1024 * 1024
        ),
    )(*(value for value, _ in inputs.values()))
    out = pl.pallas_call(
        functools.partial(result_kernel, rank),
        out_shape=tuple(jax.ShapeDtypeStruct(s, t) for s, t in outputs),
        in_specs=[smem] + [vmem] * len(middle),
        out_specs=(vmem,) * len(outputs),
        compiler_params=pltpu.CompilerParams(vmem_limit_bytes=60 * 1024 * 1024),
    )(lengths[:, 0], *parts)
    loss, query_grad, item_grad, input_grad, key_down, value_down_grad, key_up, value_up = out
    return (
        loss[0, 0],
        query_grad,
        item_grad,
        input_grad.reshape(hidden_in.shape),
        key_down.T,
        value_down_grad.T,
        key_up,
        value_up,
    )


def solution(mesh):
    in_specs = (
        P("dp", "mp"),
        P("dp", "mp"),
        P("dp"),
        P("dp", None),
        P(None, "dp", None, "mp"),
        P(None, "dp"),
        P("dp", "mp"),
        P(None, "mp"),
        P(None, "mp"),
        P("mp", "dp"),
        P(),
        P(None, "mp"),
        P(),
        P(None, "mp"),
    )
    out_specs = (
        P(),
        P("dp", "mp"),
        P("dp", "mp"),
        P(None, "dp", None, "mp"),
        P(),
        P(),
        P(None, "mp"),
        P(None, "mp"),
    )
    small = mesh.shape["mp"] == 2 and mesh.shape["dp"] == 16
    body = fused_local if small else local
    return jax.shard_map(body, mesh=mesh, in_specs=in_specs, out_specs=out_specs, check_vma=False)
```

```python
import functools
import math

import jax
import jax.numpy as jnp
from jax import lax
from jax.experimental import pallas as pl
from jax.experimental.pallas import tpu as pltpu
from jax.sharding import PartitionSpec as P

HEADS = 32
KV_HEADS = 8
HEAD_DIM = 128


INV_TEMP = 50.0
HARD_NEGATIVE_ADD = 4.0
ADAPTER_SCALE = 2.0


def final_product(left_side, right_side):
    return lax.dot_general(
        left_side, right_side, (((1,), (1,)), ((), ())), preferred_element_type=jnp.float32
    )


def first_product(left_side, right_side):
    return lax.dot_general(
        left_side, right_side, (((0,), (0,)), ((), ())), preferred_element_type=jnp.float32
    )


def local(
    query_emb,
    item_emb,
    pair_index,
    hard_index,
    hidden_in,
    lengths,
    w_query,
    key_weight_matrix,
    value_weight_matrix,
    w_out,
    key_down_matrix,
    key_up_matrix,
    value_down,
    value_up_matrix,
):
    dp_count = lax.axis_size("dp")
    local_rows = query_emb.shape[0]
    batch_size = local_rows * dp_count
    items_all = lax.all_gather(item_emb, "dp", axis=0, tiled=True)
    partial_scores = final_product(query_emb, items_all)
    pair_scores = lax.psum(partial_scores, "mp") * INV_TEMP
    columns = jnp.arange(batch_size, dtype=jnp.int32)
    hard_negative_count = jnp.sum(
        (hard_index[:, :, None] == columns[None, None, :]).astype(jnp.float32), axis=1
    )
    score_logits = pair_scores + HARD_NEGATIVE_ADD * hard_negative_count
    row_top = jnp.max(score_logits, axis=1, keepdims=True)
    log_total = row_top[:, 0] + jnp.log(jnp.sum(jnp.exp(score_logits - row_top), axis=1))
    target = (pair_index[:, None] == columns[None, :]).astype(jnp.float32)
    picked = jnp.sum(target * score_logits, axis=1)
    loss_part = jnp.sum(log_total - picked)
    residual = (jnp.exp(score_logits - log_total[:, None]) - target).astype(jnp.bfloat16)
    query_grad = (
        jnp.dot(residual, items_all, preferred_element_type=jnp.float32) * INV_TEMP
    ).astype(jnp.bfloat16)
    item_grad = lax.psum_scatter(
        first_product(residual, query_emb) * INV_TEMP, "dp", scatter_dimension=0, tiled=True
    ).astype(jnp.bfloat16)
    sub_count = hidden_in.shape[0]
    seq_len = hidden_in.shape[2]
    full_rows = lax.all_gather(hidden_in, "mp", axis=3, tiled=True)
    model_width = full_rows.shape[3]
    token_inputs = full_rows.reshape(sub_count * seq_len, model_width)
    seq_lengths = lengths[:, 0]
    last_rows = jnp.arange(sub_count, dtype=jnp.int32) * seq_len + seq_lengths - 1
    last_tokens = jnp.take(token_inputs, last_rows, axis=0)
    cot_local = item_grad[:sub_count]
    cot_full = lax.all_gather(cot_local, "mp", axis=1, tiled=True)
    adapter_rank = key_down_matrix.shape[1]
    down_both = jnp.concatenate([key_down_matrix, value_down], axis=1)
    reduced_pair = jnp.dot(token_inputs, down_both, preferred_element_type=jnp.float32).astype(
        jnp.bfloat16
    )
    reduced_key = reduced_pair[:, :adapter_rank]
    reduced_value = reduced_pair[:, adapter_rank:]
    key_rows = (
        jnp.dot(token_inputs, key_weight_matrix, preferred_element_type=jnp.float32)
        + ADAPTER_SCALE * jnp.dot(reduced_key, key_up_matrix, preferred_element_type=jnp.float32)
    ).astype(jnp.bfloat16)
    value_rows = (
        jnp.dot(token_inputs, value_weight_matrix, preferred_element_type=jnp.float32)
        + ADAPTER_SCALE
        * jnp.dot(reduced_value, value_up_matrix, preferred_element_type=jnp.float32)
    ).astype(jnp.bfloat16)
    query_width = w_query.shape[1]
    wq_full, wo_full = (
        lax.all_gather(w_query, "dp", axis=0, tiled=True),
        lax.all_gather(w_out, "dp", axis=1, tiled=True),
    )
    query = jnp.dot(last_tokens, wq_full, preferred_element_type=jnp.float32).astype(jnp.bfloat16)
    attn_grad = final_product(cot_full, wo_full).astype(jnp.bfloat16)
    group_size = HEADS // KV_HEADS
    kv_local = key_rows.shape[1] // HEAD_DIM
    score_scale = 1.0 / math.sqrt(HEAD_DIM)
    q_heads = query.reshape(sub_count, kv_local, group_size, HEAD_DIM)
    k_heads = key_rows.reshape(sub_count, seq_len, kv_local, HEAD_DIM)
    v_heads = value_rows.reshape(sub_count, seq_len, kv_local, HEAD_DIM)
    raw_scores = (
        jnp.einsum("bkgd,bjkd->bkgj", q_heads, k_heads, preferred_element_type=jnp.float32)
        * score_scale
    )
    live_mask = jnp.arange(seq_len, dtype=jnp.int32)[None, :] < seq_lengths[:, None]
    raw_scores = jnp.where(live_mask[:, None, None, :], raw_scores, -jnp.inf)
    row_peak = jnp.max(raw_scores, axis=-1, keepdims=True)
    weights = jnp.exp(raw_scores - row_peak)
    softmax_probs = weights / jnp.sum(weights, axis=-1, keepdims=True)
    prob_half = softmax_probs.astype(jnp.bfloat16)
    grad_heads = attn_grad.reshape(sub_count, kv_local, group_size, HEAD_DIM)
    prob_grad = jnp.einsum(
        "bkgd,bjkd->bkgj", grad_heads, v_heads, preferred_element_type=jnp.float32
    )
    score_grad = (
        softmax_probs
        * (prob_grad - jnp.sum(softmax_probs * prob_grad, axis=-1, keepdims=True))
        * score_scale
    ).astype(jnp.bfloat16)
    query_delta = (
        jnp.einsum("bkgj,bjkd->bkgd", score_grad, k_heads, preferred_element_type=jnp.float32)
        .astype(jnp.bfloat16)
        .reshape(sub_count, query_width)
    )
    key_adapter_change = (
        jnp.einsum("bkgj,bkgd->bjkd", score_grad, q_heads, preferred_element_type=jnp.float32)
        .astype(jnp.bfloat16)
        .reshape(sub_count * seq_len, kv_local * HEAD_DIM)
    )
    value_adapter_change = (
        jnp.einsum("bkgj,bkgd->bjkd", prob_half, grad_heads, preferred_element_type=jnp.float32)
        .astype(jnp.bfloat16)
        .reshape(sub_count * seq_len, kv_local * HEAD_DIM)
    )
    last_part = final_product(query_delta, wq_full)
    key_coefficient = final_product(key_adapter_change, key_up_matrix).astype(jnp.bfloat16)
    value_coefficient = final_product(value_adapter_change, value_up_matrix).astype(jnp.bfloat16)
    input_portion = final_product(key_adapter_change, key_weight_matrix) + final_product(
        value_adapter_change, value_weight_matrix
    )
    input_portion = input_portion + ADAPTER_SCALE * (
        final_product(key_coefficient, key_down_matrix)
        + final_product(value_coefficient, value_down)
    )
    input_portion = input_portion.at[last_rows].add(last_part)
    input_sum = lax.psum_scatter(
        input_portion.astype(jnp.bfloat16), "mp", scatter_dimension=1, tiled=True
    ).astype(jnp.float32)
    input_sum = input_sum.at[last_rows].add(cot_local.astype(jnp.float32))
    input_grad = input_sum.astype(jnp.bfloat16).reshape(hidden_in.shape)
    key_down_grad, value_down_grad = lax.psum(
        (
            ADAPTER_SCALE * first_product(token_inputs, key_coefficient),
            ADAPTER_SCALE * first_product(token_inputs, value_coefficient),
        ),
        ("dp", "mp"),
    )
    total_loss, key_up_grad, value_up_grad = lax.psum(
        (
            loss_part,
            ADAPTER_SCALE * first_product(reduced_key, key_adapter_change),
            ADAPTER_SCALE * first_product(reduced_value, value_adapter_change),
        ),
        "dp",
    )
    mean_loss = total_loss / batch_size
    return (
        mean_loss,
        query_grad,
        item_grad,
        input_grad,
        key_down_grad,
        value_down_grad,
        key_up_grad,
        value_up_grad,
    )


TILE = 1024
PLANE = 4
EMB, XS, SC, RES, QP, QZ, AP, AZ, GB, QD, LP, DN, DZ, DNG = range(14)
M_X, M_COEF, M_PART, M_LAST, M_DN = range(5)


def plain_product(left_side, right_side):
    return jnp.dot(left_side, right_side, preferred_element_type=jnp.float32)


def step_kernel(
    dp, mp, subs, rank, names, *refs,
):
    r = dict(zip(names, refs, strict=True))
    len_ref, pair_ref, hard_ref = r["lengths"], r["pair"], r["hard"]
    q_ref, item_ref, x_hbm, kup_ref, vup_ref = r["q"], r["item"], r["x"], r["kup"], r["vup"]
    xg, wq, wkv, wo, down = r["xg"], r["wq"], r["wkv"], r["wo"], r["down"]
    ssem, rsem, msend, mrecv, csem = r["ssem"], r["rsem"], r["msend"], r["mrecv"], r["csem"]
    me = lax.axis_index("dp")
    core = lax.axis_index("mp")
    other = 1 - core
    rows, feats = x_hbm.shape
    seq_len = rows // subs
    local_rows = q_ref.shape[0]
    batch = dp * local_rows
    dq, qw = wq.shape
    kw = wkv.shape[1] // 2
    tiles = feats // TILE
    per_core = dp // mp
    home = me // per_core
    slot = lax.rem(me, per_core)
    at_home = core == home
    mesh_id = pl.DeviceIdType.MESH
    f32, bf16 = jnp.float32, jnp.bfloat16

    local_copies = [
        pltpu.make_async_copy(src, dst, csem.at[i])
        for i, (src, dst) in enumerate(
            (
                (x_hbm, xg.at[core]),
                (r["wq_hbm"], wq),
                (r["wk_hbm"], wkv.at[:, pl.ds(0, kw)]),
                (r["wv_hbm"], wkv.at[:, pl.ds(kw, kw)]),
                (r["wo_hbm"], wo),
                (r["kdown"], down.at[pl.ds(0, rank)]),
                (r["vdown"], down.at[pl.ds(rank, rank)]),
            )
        )
    ]
    for copy in local_copies:
        copy.start()

    barrier = pltpu.get_barrier_semaphore()

    @pl.loop(1, dp * mp)
    def _(n):
        flat = lax.rem(me * mp + core + n, dp * mp)
        pl.semaphore_signal(
            barrier, inc=1, device_id=(flat // mp, lax.rem(flat, mp)), device_id_type=mesh_id
        )

    es, emb_land = r["es"], r["emb_land"]
    both = jnp.concatenate([q_ref[...].astype(f32), item_ref[...].astype(f32)], axis=0)
    for c in range(per_core):
        es[c] = both[:, c * dq : (c + 1) * dq].astype(bf16)
    pl.semaphore_wait(barrier, dp * mp - 1)

    def remote(source, landing, send, recv, target, target_core):
        return pltpu.make_async_remote_copy(
            src_ref=source,
            dst_ref=landing,
            send_sem=send,
            recv_sem=recv,
            device_id=(target, target_core),
            device_id_type=mesh_id,
        )

    def slice_copy(op, n, source, landing):
        return remote(
            source.at[n // mp], landing.at[me], ssem.at[op], rsem.at[op],
            core * per_core + n // mp, lax.rem(n, mp),
        )

    def is_self(n):
        return (core * per_core + n // mp == me) & (lax.rem(n, mp) == core)

    def slice_start(op, source, landing):
        @pl.loop(0, dp)
        def _(n):
            @pl.when(jnp.logical_not(is_self(n)))
            def _():
                slice_copy(op, n, source, landing).start()

        @pl.when(at_home)
        def _():
            landing[me] = source[slot]

    def arrived(op, landing, count):
        some = landing.at[pl.ds(0, count)]
        remote(some, some, ssem.at[op], rsem.at[op], me, other).wait_recv()

    def departed(op, landing, count):
        some = landing.at[pl.ds(0, count)]
        remote(some, some, ssem.at[op], rsem.at[op], me, other).wait_send()

    def by_home(wait, op, landing, count):
        @pl.when(at_home)
        def _():
            wait(op, landing, count - 1)

        @pl.when(jnp.logical_not(at_home))
        def _():
            wait(op, landing, count)

    def dp_copy(op, k, source, landing):
        target = lax.rem(me + k, dp)
        return remote(
            source(target), landing.at[me], ssem.at[op], rsem.at[op], target, core
        )

    def dp_start(op, source, landing):
        @pl.loop(1, dp, unroll=True)
        def _(k):
            dp_copy(op, k, source, landing).start()

    def dp_wait(op, source, landing):
        arrived(op, landing, dp - 1)

    def mp_copy(op, source, landing):
        return remote(source, landing, msend.at[op], mrecv.at[op], me, other)

    def total_of(landing):
        total = landing[0].astype(f32)
        for j in range(1, landing.shape[0]):
            total = total + landing[j].astype(f32)
        return total

    spot_in_plane, level = lax.rem(me, PLANE), me // PLANE
    levels = dp // PLANE

    def plane_start(op, source, landing):
        for k in range(1, PLANE):
            to = lax.rem(spot_in_plane + k, PLANE)
            remote(
                source.at[to], landing.at[spot_in_plane], ssem.at[op], rsem.at[op],
                level * PLANE + to, core,
            ).start()
        landing[spot_in_plane] = source[spot_in_plane]

    def line_start(op, plane_op, plane_landing, source, landing):
        arrived(plane_op, plane_landing, PLANE - 1)
        source[...] = total_of(plane_landing)
        for k in range(1, levels):
            to = lax.rem(level + k, levels)
            remote(
                source.at[to], landing.at[level], ssem.at[op], rsem.at[op],
                to * PLANE + spot_in_plane, core,
            ).start()
        landing[level] = source[level]

    def line_total(op, landing):
        arrived(op, landing, levels - 1)
        return total_of(landing)

    emb_args = (EMB, es, emb_land)
    slice_start(*emb_args)

    local_copies[0].wait()
    last = [jnp.clip(len_ref[b] - 1, 0, seq_len - 1) + b * seq_len for b in range(subs)]
    one_row = lax.broadcasted_iota(jnp.int32, (8, rows), 0)
    one_col = lax.broadcasted_iota(jnp.int32, (8, rows), 1)
    picked_rows = jnp.zeros((8, rows), f32)
    for b in range(subs):
        picked_rows = jnp.where((one_row == b) & (one_col == last[b]), 1.0, picked_rows)
    last_tokens = plain_product(picked_rows.astype(bf16), xg[core])[:subs]
    xs, x_land = r["xs"], r["x_land"]
    for c in range(per_core):
        xs[c] = last_tokens[:, c * dq : (c + 1) * dq]
    xs_args = (XS, xs, x_land)
    slice_start(*xs_args)
    x_copy = mp_copy(M_X, xg.at[core], xg.at[core])
    x_copy.start()

    by_home(arrived, EMB, emb_land, dp)
    emb = emb_land[...].astype(f32)
    queries = emb[:, :local_rows].reshape(batch, dq).astype(bf16)
    items = emb[:, local_rows:].reshape(batch, dq).astype(bf16)
    sc, sc_land = r["sc"], r["sc_land"]
    sc[...] = final_product(queries, items).reshape(dp, local_rows, batch)
    sc_args = (SC, lambda t: sc.at[t], sc_land)
    dp_start(*sc_args)
    sc_land[me] = sc[me]

    by_home(arrived, XS, x_land, dp)
    x_rows = r["x_rows"]
    for j in range(dp):
        x_rows[j * subs : (j + 1) * subs, :] = x_land[j]
    local_copies[1].wait()
    part_q, plane_q, line_q, land_q = r["part_q"], r["plane_q"], r["line_q"], r["land_q"]
    query_part = plain_product(x_rows[...].astype(bf16), wq[...])
    for j in range(dp):
        part_q[j % PLANE, j // PLANE] = query_part[j * subs : (j + 1) * subs]

    columns = lax.broadcasted_iota(jnp.int32, (local_rows, batch), 1)
    row_ids = lax.broadcasted_iota(jnp.int32, (local_rows, batch), 0)
    hard_count = jnp.zeros((local_rows, batch), f32)
    target = jnp.zeros((local_rows, batch), f32)
    for i in range(local_rows):
        for h in range(hard_ref.shape[0]):
            hit = (row_ids == i) & (columns == hard_ref[h, i])
            hard_count = hard_count + jnp.where(hit, 1.0, 0.0)
        target = jnp.where((row_ids == i) & (columns == pair_ref[i]), 1.0, target)
    dp_wait(*sc_args)
    logits = total_of(sc_land) * INV_TEMP + HARD_NEGATIVE_ADD * hard_count
    row_top = jnp.max(logits, axis=1, keepdims=True)
    log_total = row_top + jnp.log(jnp.sum(jnp.exp(logits - row_top), axis=1, keepdims=True))
    picked = jnp.sum(target * logits, axis=1, keepdims=True)
    loss_part = jnp.sum(log_total - picked, axis=0, keepdims=True)
    residual = (jnp.exp(logits - log_total) - target).astype(bf16).astype(f32)
    res_own, res_land = r["res_own"], r["res_land"]
    res_own[...] = residual
    res_args = (RES, lambda t: res_own, res_land)
    dp_start(*res_args)
    res_land[me] = residual
    plane_start(QP, part_q, plane_q)

    for i in (2, 3, 5, 6):
        local_copies[i].wait()

    def project(which):
        spot = pl.ds(pl.multiple_of(which * feats, feats), feats)
        block = xg[which]
        return plain_product(block, wkv[spot, :]), final_product(block, down[:, spot])

    acc, acc_low = r["acc"], r["acc_low"]
    acc[...], acc_low[...] = project(core)
    line_start(QZ, QP, plane_q, line_q, land_q)

    dp_wait(*res_args)
    res = res_land[...].reshape(batch, batch)
    query_grad = plain_product(res.astype(bf16), items) * INV_TEMP
    item_grad = (plain_product(res.T.astype(bf16), queries) * INV_TEMP).astype(bf16).astype(f32)
    item_slabs = item_grad.reshape(dp, local_rows, dq)
    cot_rows = r["cot_rows"]
    for j in range(dp):
        cot_rows[j * subs : (j + 1) * subs, :] = item_slabs[j, :subs]
    local_copies[4].wait()
    part_a, plane_a, line_a, land_a = r["part_a"], r["plane_a"], r["line_a"], r["land_a"]
    grad_part = final_product(cot_rows[...].astype(bf16), wo[...])
    for j in range(dp):
        part_a[j % PLANE, j // PLANE] = grad_part[j * subs : (j + 1) * subs]
    plane_start(AP, part_a, plane_a)
    gs, g_land = r["gs"], r["g_land"]
    gs[...] = jnp.concatenate(
        [query_grad.reshape(dp, local_rows, dq), item_slabs], axis=1
    ).astype(bf16)

    def back_copy(k):
        to = lax.rem(me + k, dp)
        return remote(gs.at[to], g_land.at[slot], ssem.at[GB], rsem.at[GB], to, core)

    @pl.when(at_home)
    def _():
        @pl.loop(1, dp)
        def _(k):
            back_copy(k).start()

        g_land[slot] = gs[me]

    x_copy.wait()
    more, more_low = project(other)
    line_start(AZ, AP, plane_a, line_a, land_a)
    low = (acc_low[...] + more_low).astype(bf16)
    low_key, low_value = low[:, :rank], low[:, rank:]
    key_part, value_part = acc[:, :kw] + more[:, :kw], acc[:, kw:] + more[:, kw:]
    keys = (key_part + ADAPTER_SCALE * plain_product(low_key, kup_ref[...])).astype(bf16)
    values = (value_part + ADAPTER_SCALE * plain_product(low_value, vup_ref[...])).astype(bf16)

    heads = qw // HEAD_DIM
    group_size = HEADS // KV_HEADS
    score_scale = 1.0 / math.sqrt(HEAD_DIM)

    def spread(flat, blocks):
        blocks[...] = jnp.zeros_like(blocks)
        for b in range(subs):
            for h in range(heads):
                kv = h // group_size * HEAD_DIM
                blocks[b * heads + h : b * heads + h + 1, kv : kv + HEAD_DIM] = flat[
                    b : b + 1, h * HEAD_DIM : (h + 1) * HEAD_DIM
                ]
        return blocks[...].astype(bf16)

    r["flat_q"][...] = line_total(QZ, land_q).astype(bf16).astype(f32)
    q_half = spread(r["flat_q"], r["q_blk"])
    raw = final_product(q_half, keys) * score_scale
    head_rows = lax.broadcasted_iota(jnp.int32, raw.shape, 0)
    token_ids = lax.broadcasted_iota(jnp.int32, raw.shape, 1)
    live = jnp.zeros(raw.shape, jnp.bool_)
    for b in range(subs):
        mine = (head_rows >= b * heads) & (head_rows < (b + 1) * heads)
        live = live | (mine & (token_ids >= b * seq_len) & (token_ids <= last[b]))
    raw = jnp.where(live, raw, -jnp.inf)
    weights = jnp.exp(raw - jnp.max(raw, axis=1, keepdims=True))
    probs = weights / jnp.sum(weights, axis=1, keepdims=True)
    r["flat_a"][...] = line_total(AZ, land_a).astype(bf16).astype(f32)
    g_half = spread(r["flat_a"], r["g_blk"])
    prob_grad = final_product(g_half, values)
    score_grad = (
        probs * (prob_grad - jnp.sum(probs * prob_grad, axis=1, keepdims=True)) * score_scale
    ).astype(bf16)

    key_delta = first_product(score_grad, q_half).astype(bf16)
    value_delta = first_product(probs.astype(bf16), g_half).astype(bf16)
    coef = jnp.concatenate(
        [final_product(key_delta, kup_ref[...]), final_product(value_delta, vup_ref[...])], axis=1
    ).astype(bf16)
    coef_g = r["coef_g"]
    coef_g[core] = coef
    coef_copy = mp_copy(M_COEF, coef_g.at[core], coef_g.at[core])
    coef_copy.start()

    query_delta = plain_product(score_grad, keys)
    qd_f, qd_own, qd_all = r["qd_f"], r["qd_own"], r["qd_all"]
    blocks = qw // dq
    in_block = dq // HEAD_DIM
    for b in range(subs):
        for h in range(heads):
            kv = h // group_size * HEAD_DIM
            spot = b * blocks + h // in_block
            lane = h % in_block * HEAD_DIM
            qd_f[spot : spot + 1, lane : lane + HEAD_DIM] = query_delta[
                b * heads + h : b * heads + h + 1, kv : kv + HEAD_DIM
            ]
    qd_own[...] = qd_f[...].astype(bf16)
    qd_args = (QD, lambda t: qd_own, qd_all)
    dp_start(*qd_args)
    qd_all[me] = qd_own[...]

    dn, dn_plane, dn_line, dn_land = r["dn"], r["dn_plane"], r["dn_line"], r["dn_land"]
    dn_all = r["dn_all"]
    up_grad = ADAPTER_SCALE * jnp.concatenate(
        [first_product(low_key, key_delta), first_product(low_value, value_delta)], axis=0
    )
    lane_groups = up_grad.shape[1] // 128
    cols = feats // dp
    own_down = first_product(coef, xg[core])
    for j in range(dp):
        top = j // lane_groups * 8
        lane = j % lane_groups * 128
        dn[j % PLANE, j // PLANE, 2 * rank :, :] = up_grad[top : top + 8, lane : lane + 128]
    coef_copy.wait()
    down_part = ADAPTER_SCALE * (own_down + first_product(coef_g[other], xg[core]))
    for j in range(dp):
        dn[j % PLANE, j // PLANE, : 2 * rank, :] = down_part[:, j * cols : (j + 1) * cols]
    plane_start(DN, dn, dn_plane)

    pacc, pbuf, p_land, last_f = r["pacc"], r["pbuf"], r["p_land"], r["last_f"]
    deltas = jnp.concatenate([key_delta, value_delta], axis=1)

    def portion(which, place, finish):
        @pl.loop(0, tiles)
        def _(t):
            cols = pl.ds(pl.multiple_of(t * TILE, TILE), TILE)
            spot = pl.ds(pl.multiple_of(which * feats + t * TILE, TILE), TILE)
            pacc[...] = final_product(deltas, wkv[spot, :]) + ADAPTER_SCALE * plain_product(
                coef, down[:, spot]
            )
            for b in range(subs):
                last_f[place, b : b + 1, cols] = pacc[pl.ds(last[b], 1), :]
            finish(cols, pacc[...].astype(bf16))

    def to_other(cols, share):
        pbuf[:, cols] = share

    portion(other, 1, to_other)
    part_copy = mp_copy(M_PART, pbuf, p_land)
    part_copy.start()

    line_start(DZ, DN, dn_plane, dn_line, dn_land)

    dp_wait(*qd_args)
    changes = qd_all[...].reshape(dp * subs * blocks, dq)
    block_ids = lax.rem(lax.broadcasted_iota(jnp.int32, (dp * subs * blocks, dq), 0), blocks)
    last_part = jnp.zeros((dp * subs * blocks, dq), f32)
    for c in range(blocks):
        term = final_product(changes, wq[:, c * dq : (c + 1) * dq])
        last_part = jnp.where(block_ids == c, term, last_part)
    last_part = jnp.sum(last_part.reshape(dp * subs, blocks, dq), axis=1)
    lp, lp_land = r["lp"], r["lp_land"]
    for j in range(dp):
        lp[j, :subs] = last_part[j * subs : (j + 1) * subs]
        lp[j, subs:] = jnp.broadcast_to(loss_part, (lp.shape[1] - subs, dq))
    lp_args = (LP, lambda t: lp.at[t], lp_land)
    dp_start(*lp_args)
    lp_land[me] = lp[me]

    dn_sum = line_total(DZ, dn_land)
    dn_all[core, me] = jnp.concatenate([dn_sum, jnp.zeros((8, cols), f32)], 0).astype(bf16)
    dng_args = (DNG, lambda t: dn_all.at[core, me], dn_all.at[core])
    dp_start(*dng_args)


    part_copy.wait()

    def to_sum(cols, share):
        r["input_sum"][:, cols] = (share.astype(f32) + p_land[:, cols].astype(f32)).astype(bf16)

    portion(core, 0, to_sum)

    by_home(arrived, GB, g_land, per_core)

    dp_wait(*lp_args)
    last_total, last_send, last_land = r["last_total"], r["last_send"], r["last_land"]
    loss = lp_land[0, subs : subs + 1, 0:1]
    for j in range(1, dp):
        loss = loss + lp_land[j, subs : subs + 1, 0:1]
    r["loss"][...] = loss / batch
    for which in range(mp):
        for c in range(per_core):
            last_total[which, :, c * dq : (c + 1) * dq] = lp_land[which * per_core + c, :subs]
    last_send[...] = (last_f[1] + last_total[other]).astype(bf16).astype(f32)
    last_copy = mp_copy(M_LAST, last_send, last_land)
    last_copy.start()
    dp_wait(*dng_args)
    down_copy = mp_copy(M_DN, dn_all.at[core], dn_all.at[core])
    down_copy.start()

    own_last = (last_f[0] + last_total[core]).astype(bf16).astype(f32)
    last_copy.wait()
    r["last_sum"][...] = own_last + last_land[...]
    for j in range(dp):
        r["up_all"][j] = dn_all[core, j, 2 * rank :, :]
    down_copy.wait()

    by_home(departed, EMB, emb_land, dp)
    by_home(departed, XS, x_land, dp)

    @pl.when(at_home)
    def _():
        departed(GB, gs, dp - 1)

    for op, _, landing in (sc_args, res_args, qd_args, lp_args, dng_args):
        departed(op, landing, dp - 1)
    for op, landing in ((QP, plane_q), (AP, plane_a), (DN, dn_plane)):
        departed(op, landing, PLANE - 1)
    for op, landing in ((QZ, land_q), (AZ, land_a), (DZ, dn_land)):
        departed(op, landing, levels - 1)


def result_kernel(
    rank, len_ref, loss_sum, g_land, input_sum, last_sum, dn_all, up_all,
    loss, q_grad, item_grad, input_grad, key_down, value_down, key_up, value_up,
):
    f32, bf16 = jnp.float32, jnp.bfloat16
    mp, dp, _, cols = dn_all.shape
    per_core, group_rows, dq = g_land.shape
    local_rows = group_rows // 2
    subs, feats = last_sum.shape
    rows = input_sum.shape[0]
    seq_len = rows // subs
    loss[...] = loss_sum[...]
    ids = lax.broadcasted_iota(jnp.int32, (rows, dq), 0)
    for c in range(per_core):
        span = slice(c * dq, (c + 1) * dq)
        slab = g_land[c].astype(f32)
        q_grad[:, span] = slab[:local_rows].astype(bf16)
        item_grad[:, span] = slab[local_rows:].astype(bf16)
        ends = last_sum[:, span] + slab[local_rows : local_rows + subs]
        tokens = input_sum[:, span].astype(f32)
        for b in range(subs):
            last = jnp.clip(len_ref[b] - 1, 0, seq_len - 1) + b * seq_len
            tokens = jnp.where(ids == last, ends[b : b + 1], tokens)
        input_grad[:, span] = tokens.astype(bf16)
    lane_groups = key_up.shape[1] // 128
    for j in range(dp):
        top = j // lane_groups * 8
        lane = j % lane_groups * 128
        out = key_up if top < rank else value_up
        slab = up_all[j].astype(f32)
        out[top % rank : top % rank + 8, lane : lane + 128] = slab[:8]
    for which in range(mp):
        for j in range(dp):
            span = slice(which * feats + j * cols, which * feats + (j + 1) * cols)
            slab = dn_all[which, j, : 2 * rank, :].astype(f32)
            key_down[:, span] = slab[:rank]
            value_down[:, span] = slab[rank:]


def fused_local(
    query_emb, item_emb, pair_index, hard_index, hidden_in, lengths, w_query, key_weight_matrix,
    value_weight_matrix, w_out, key_down_matrix, key_up_matrix, value_down, value_up_matrix,
):
    dp, mp = lax.axis_size("dp"), lax.axis_size("mp")
    local_rows, feats = query_emb.shape
    subs, _, seq_len, _ = hidden_in.shape
    rows = subs * seq_len
    rank, kw = key_up_matrix.shape
    dq, qw = w_query.shape
    width = feats * mp
    heads = qw // HEAD_DIM
    batch = dp * local_rows
    per_core = dp // mp
    levels = dp // PLANE
    blocks = qw // dq
    slab = 2 * rank + 16
    f32, bf16 = jnp.float32, jnp.bfloat16
    vmem, hbm = pl.BlockSpec(memory_space=pltpu.VMEM), pl.BlockSpec(memory_space=pl.ANY)
    smem = pl.BlockSpec(memory_space=pltpu.SMEM)
    inputs = {
        "lengths": (lengths[:, 0], smem),
        "pair": (pair_index, smem),
        "hard": (hard_index.T, smem),
        "q": (query_emb, vmem),
        "item": (item_emb, vmem),
        "x": (hidden_in.reshape(rows, feats), hbm),
        "wq_hbm": (w_query, hbm),
        "wk_hbm": (key_weight_matrix, hbm),
        "wv_hbm": (value_weight_matrix, hbm),
        "wo_hbm": (w_out, hbm),
        "kdown": (key_down_matrix.T, hbm),
        "vdown": (value_down.T, hbm),
        "kup": (key_up_matrix, vmem),
        "vup": (value_up_matrix, vmem),
    }
    middle = {
        "loss": ((1, 1), f32),
        "g_land": ((per_core, 2 * local_rows, dq), bf16),
        "input_sum": ((rows, feats), bf16),
        "last_sum": ((subs, feats), f32),
        "dn_all": ((mp, dp, slab, feats // dp), bf16),
        "up_all": ((dp, 16, 128), bf16),
    }
    outputs = (
        ((1, 1), f32),
        ((local_rows, feats), bf16),
        ((local_rows, feats), bf16),
        ((rows, feats), bf16),
        ((rank, width), f32),
        ((rank, width), f32),
        ((rank, kw), f32),
        ((rank, kw), f32),
    )
    scratch = {
        "es": ((per_core, 2 * local_rows, dq), bf16),
        "emb_land": ((dp, 2 * local_rows, dq), bf16),
        "xs": ((per_core, subs, dq), f32),
        "x_land": ((dp, subs, dq), f32),
        "x_rows": ((dp * subs, dq), f32),
        "sc": ((dp, local_rows, batch), f32),
        "sc_land": ((dp, local_rows, batch), f32),
        "res_own": ((local_rows, batch), f32),
        "res_land": ((dp, local_rows, batch), f32),
        "part_q": ((PLANE, levels, subs, qw), f32),
        "plane_q": ((PLANE, levels, subs, qw), f32),
        "line_q": ((levels, subs, qw), f32),
        "land_q": ((levels, subs, qw), f32),
        "cot_rows": ((dp * subs, dq), f32),
        "part_a": ((PLANE, levels, subs, qw), f32),
        "plane_a": ((PLANE, levels, subs, qw), f32),
        "line_a": ((levels, subs, qw), f32),
        "land_a": ((levels, subs, qw), f32),
        "gs": ((dp, 2 * local_rows, dq), bf16),
        "xg": ((mp, rows, feats), bf16),
        "wq": ((dq, qw), bf16),
        "wkv": ((width, 2 * kw), bf16),
        "wo": ((qw, dq), bf16),
        "down": ((2 * rank, width), bf16),
        "acc": ((rows, 2 * kw), f32),
        "acc_low": ((rows, 2 * rank), f32),
        "q_blk": ((subs * heads, kw), f32),
        "g_blk": ((subs * heads, kw), f32),
        "flat_q": ((subs, qw), f32),
        "flat_a": ((subs, qw), f32),
        "qd_f": ((subs * blocks, dq), f32),
        "qd_own": ((subs * blocks, dq), bf16),
        "qd_all": ((dp, subs * blocks, dq), bf16),
        "lp": ((dp, 2 * subs, dq), f32),
        "lp_land": ((dp, 2 * subs, dq), f32),
        "coef_g": ((mp, rows, 2 * rank), bf16),
        "pacc": ((rows, TILE), f32),
        "pbuf": ((rows, feats), bf16),
        "p_land": ((rows, feats), bf16),
        "last_f": ((2, subs, feats), f32),
        "last_total": ((mp, subs, feats), f32),
        "last_send": ((subs, feats), f32),
        "last_land": ((subs, feats), f32),
        "dn": ((PLANE, levels, slab - 8, feats // dp), f32),
        "dn_plane": ((PLANE, levels, slab - 8, feats // dp), f32),
        "dn_line": ((levels, slab - 8, feats // dp), f32),
        "dn_land": ((levels, slab - 8, feats // dp), f32),
    }
    sems = {"ssem": (14,), "rsem": (14,), "msend": (5,), "mrecv": (5,), "csem": (7,)}
    names = (*inputs, *middle, *scratch, *sems)
    parts = pl.pallas_call(
        functools.partial(step_kernel, dp, mp, subs, rank, names),
        out_shape=tuple(jax.ShapeDtypeStruct(s, t) for s, t in middle.values()),
        in_specs=[spec for _, spec in inputs.values()],
        out_specs=(vmem,) * len(middle),
        scratch_shapes=[pltpu.VMEM(s, t) for s, t in scratch.values()]
        + [pltpu.SemaphoreType.DMA(s) for s in sems.values()],
        compiler_params=pltpu.CompilerParams(
            collective_id=0, has_side_effects=True, vmem_limit_bytes=60 * 1024 * 1024
        ),
    )(*(value for value, _ in inputs.values()))
    out = pl.pallas_call(
        functools.partial(result_kernel, rank),
        out_shape=tuple(jax.ShapeDtypeStruct(s, t) for s, t in outputs),
        in_specs=[smem] + [vmem] * len(middle),
        out_specs=(vmem,) * len(outputs),
        compiler_params=pltpu.CompilerParams(vmem_limit_bytes=60 * 1024 * 1024),
    )(lengths[:, 0], *parts)
    loss, query_grad, item_grad, input_grad, key_down, value_down_grad, key_up, value_up = out
    return (
        loss[0, 0],
        query_grad,
        item_grad,
        input_grad.reshape(hidden_in.shape),
        key_down.T,
        value_down_grad.T,
        key_up,
        value_up,
    )


def solution(mesh):
    in_specs = (
        P("dp", "mp"),
        P("dp", "mp"),
        P("dp"),
        P("dp", None),
        P(None, "dp", None, "mp"),
        P(None, "dp"),
        P("dp", "mp"),
        P(None, "mp"),
        P(None, "mp"),
        P("mp", "dp"),
        P(),
        P(None, "mp"),
        P(),
        P(None, "mp"),
    )
    out_specs = (
        P(),
        P("dp", "mp"),
        P("dp", "mp"),
        P(None, "dp", None, "mp"),
        P(),
        P(),
        P(None, "mp"),
        P(None, "mp"),
    )
    small = mesh.shape["mp"] == 2 and mesh.shape["dp"] == 16
    body = fused_local if small else local
    return jax.shard_map(body, mesh=mesh, in_specs=in_specs, out_specs=out_specs, check_vma=False)
```
